512 devices in a mesh: seg: 32 (over y, x), step: 16 (over z, core).
Axes of the slice: x: 4, y: 8, z: 8, core: 2. Of those that a mesh axis runs over, the one named last changes fastest.
Arguments:
- trajectory: bfloat16 [16, 4096, 1536], P('step', 'seg'), may hold values from -6 to 6
- noise: bfloat16 [4096, 1536], P('seg'), may hold values from -6 to 6
- mod_shift: float32 [16, 1536], P('step'), may hold values from -3 to 3
- mod_scale: float32 [16, 1536], P('step'), may hold values from -2.5 to 2.5
- step_size: float32 [16], P('step'), may hold values from 0.2 to 0.6
- prompt_table: float32 [8, 1536], replicated, may hold values from -6 to 6
- prompt_map: int32 [4096], P('seg'), may hold values from 0 to 7
- w_qkv: bfloat16 [1536, 2304], P(('seg', 'step')), as said below
- w_out: bfloat16 [768, 1536], P(None, 'step'), may hold values from -0.21875 to 0.21875
Outputs:
- new_trajectory: bfloat16 [16, 4096, 1536], P('step', 'seg')
The draws below stay inside these ranges and needn't reach their ends.
Inputs may be any that keep to these rules, and one draw needn't show every extreme that they name: `w_qkv`: columns for queries, keys and values of 12 heads.
All inputs are finite; a program needn't handle non-finite values.
Results may differ from the reference program's by a relative error of at most 0.011.
Values may be sent and summed in bfloat16 or wider, within the bound.
A program may use at most 64 MiB of HBM per device.

```python
import math
import jax
import jax.numpy as jnp
from jax import lax

D = 1536
HEADS = 12
HEAD_DIM = 64
PROMPTS = 8
L_DEV = 128
HALO = 64
HQ = 768
STEPS = 16
FRAMES = 4096


def draw_w_qkv(key, part):
    key = jax.random.fold_in(key, 11)
    key_q, key_k, key_v = jax.random.split(key, 3)
    width = HEADS * HEAD_DIM
    base = D ** (-0.5)
    queries = jax.random.normal(key_q, (D, width), jnp.float32) * base
    values = jax.random.normal(key_v, (D, width), jnp.float32) * (6.0 * base)
    keys = jax.random.normal(key_k, (D, width), jnp.float32) * base
    return jnp.concatenate([queries, keys, values], axis=1).astype(jnp.bfloat16)


def touch_ends(drawn, key, low, high):
    longest = drawn.shape.index(max(drawn.shape))
    spots = []
    for shift in (0, 1):
        where = [jax.random.randint(jax.random.fold_in(key, axis), (), 0, length) for axis, length in enumerate(drawn.shape)]
        where[longest] = (where[longest] + shift) % drawn.shape[longest]
        spots.append(tuple(where))
    return drawn.at[spots[0]].set(low).at[spots[1]].set(high)


def block_levels(stream_key, shape, cuts, least, high):
    def one(axis_at, shards_of):
        heights = jax.random.uniform(jax.random.fold_in(jax.random.fold_in(stream_key, 6), axis_at), (shards_of,), jnp.float32, least / len(cuts), high / len(cuts))
        return jnp.repeat(jnp.exp(heights), shape[axis_at] // shards_of).reshape((-1,) + (1,) * (len(shape) - axis_at - 1))

    factor_of = one(*cuts[0])
    for cut in cuts[1:]:
        factor_of = factor_of * one(*cut)
    return factor_of


def centred(key, extent, scale, limit, cuts=(), kind=jnp.bfloat16):
    loudness = block_levels(key, extent, cuts, -0.22, 0.18) if cuts else 1.0
    drawn = jax.random.normal(key, extent, jnp.float32) * scale * loudness
    return jnp.minimum(jnp.maximum(drawn, -limit), limit).astype(kind)


def setup_inputs(seed: int = 0) -> dict:
    splits = jax.random.split(jax.random.key(seed), 10)
    return {
        "trajectory": centred(splits[0], (STEPS, FRAMES, D), 1.0, 6.0, ((0, 16), (1, 32))),
        "noise": centred(splits[1], (FRAMES, D), 1.0, 6.0, ((0, 32),)),
        "mod_shift": centred(splits[2], (STEPS, D), 0.5, 3.0, ((0, 16),), jnp.float32),
        "mod_scale": centred(splits[3], (STEPS, D), 0.3, 2.5, ((0, 16),), jnp.float32),
        "step_size": jnp.clip(jnp.exp(math.log(0.6) - 1.0986123 * jax.random.uniform(splits[4], (STEPS,), jnp.float32) ** block_levels(splits[4], (STEPS,), ((0, 16),), -0.2, 0.2)), 0.2, 0.6),
        "prompt_table": centred(splits[5], (PROMPTS, D), 1.0, 6.0, (), jnp.float32),
        "prompt_map": touch_ends(jax.random.randint(splits[6], (FRAMES,), 0, PROMPTS), jax.random.fold_in(splits[6], 1), 0, PROMPTS - 1).astype(jnp.int32),
        "w_qkv": draw_w_qkv(jax.random.fold_in(splits[9], 71), 0),
        "w_out": centred(splits[8], (HQ, D), HQ ** -0.5, 0.21875, ((1, 16),)),
    }


def window_attention(queries, keys, values, first_row, frames_all):
    row_count = queries.shape[0]
    key_count = keys.shape[0]
    halo_width = (key_count - row_count) // 2
    query_pos = first_row + jnp.arange(row_count, dtype=jnp.int32)
    key_pos = first_row - halo_width + jnp.arange(key_count, dtype=jnp.int32)
    distance = key_pos[None, :] - query_pos[:, None]
    allowed = (jnp.abs(distance) <= halo_width) & (key_pos[None, :] >= 0) & (key_pos[None, :] < frames_all)
    head_count = queries.shape[1] // HEAD_DIM
    q_heads = queries.reshape(row_count, head_count, HEAD_DIM).transpose(1, 0, 2)
    k_heads = keys.reshape(key_count, head_count, HEAD_DIM).transpose(1, 0, 2)
    v_heads = values.reshape(key_count, head_count, HEAD_DIM).transpose(1, 0, 2)

    def one_head(pieces):
        q_head, k_head, v_head = pieces
        scores = jnp.dot(q_head, k_head.T, preferred_element_type=jnp.float32) * 0.125
        scores = jnp.where(allowed, scores, jnp.float32(-1e+30))
        largest = lax.optimization_barrier(jnp.max(scores, axis=1, keepdims=True))
        lifted = jnp.exp(scores - largest)
        weights = (lifted / lax.optimization_barrier(jnp.sum(lifted, axis=1, keepdims=True))).astype(jnp.bfloat16)
        return jnp.dot(weights, v_head, preferred_element_type=jnp.float32).astype(jnp.bfloat16)
    attended = lax.map(one_head, (q_heads, k_heads, v_heads))
    return attended.transpose(1, 0, 2).reshape(row_count, head_count * HEAD_DIM)

def modulate(latent, chosen, shift_row, scale_row):
    inputs = latent.astype(jnp.float32) + chosen
    center = lax.optimization_barrier(jnp.mean(inputs, axis=-1, keepdims=True))
    spread = lax.optimization_barrier(jnp.mean(jnp.square(inputs - center), axis=-1, keepdims=True))
    normed = (inputs - center) * lax.rsqrt(spread + 1e-06)
    return (normed * (1.0 + scale_row) + shift_row).astype(jnp.bfloat16)

def reference(trajectory, noise, mod_shift, mod_scale, step_size, prompt_table, prompt_map, w_qkv, w_out):
    frames_all = noise.shape[0]
    hidden_width = w_out.shape[0]
    chosen = prompt_table[prompt_map]

    def drift_of(latent, shift_row, scale_row):
        modulated = modulate(latent, chosen, shift_row, scale_row)
        qkv = jnp.dot(modulated, w_qkv, preferred_element_type=jnp.float32).astype(jnp.bfloat16)
        queries = qkv[:, :hidden_width]
        padded = jnp.pad(qkv[:, hidden_width:], ((HALO, HALO), (0, 0)))

        def block_fn(block_index):
            first_row = block_index * L_DEV
            q_block = lax.dynamic_slice_in_dim(queries, first_row, L_DEV, 0)
            kv_block = lax.dynamic_slice_in_dim(padded, first_row, L_DEV + 2 * HALO, 0)
            return window_attention(q_block, kv_block[:, :hidden_width], kv_block[:, hidden_width:], first_row, frames_all)
        attended = lax.map(block_fn, jnp.arange(frames_all // L_DEV, dtype=jnp.int32))
        attended = attended.reshape(frames_all, hidden_width)
        return jnp.dot(attended, w_out, preferred_element_type=jnp.float32)

    def advance(prefix, pieces):
        latent, shift_row, scale_row, size_row = pieces
        updated = (noise.astype(jnp.float32) + prefix).astype(jnp.bfloat16)
        drift_field = drift_of(latent, shift_row, scale_row)
        return (prefix + size_row * drift_field, updated)
    start_sum = jnp.zeros(noise.shape, jnp.float32)
    final_sum, result = lax.scan(advance, start_sum, (trajectory, mod_shift, mod_scale, step_size))
    return result
```

```python
import functools

import jax
import jax.numpy as jnp
from jax import lax
from jax.experimental import pallas as pl
from jax.experimental.pallas import tpu as pltpu
from jax.sharding import PartitionSpec as P

MESH = pl.DeviceIdType.MESH
BF16 = jnp.bfloat16
F32 = jnp.float32
XN, YN, ZN = 4, 8, 8
SEGS, STEPS = XN * YN, 2 * ZN
ROWS, HALO, D, HQ = 128, 64, 1536, 768
KEYS = ROWS + 2 * HALO
HALF = HQ // 2
CHUNKS = 9
SHARD = 3
BLOCK = SHARD * STEPS
SLOT = 32
CUT = 512
WO = D // STEPS
SEMS = 160


def dot(a, b, contract=((1,), (0,)), precision=None):
    return lax.dot_general(a, b, (contract, ((), ())), preferred_element_type=F32, precision=precision)


class Net:
    def __init__(self, send, recv):
        self.sems, self.index, self.sent = (send, recv), {}, []

    def copy(self, key, src, dst, device):
        at = self.index.setdefault(key, len(self.index))
        send, recv = self.sems
        return pltpu.make_async_remote_copy(
            src_ref=src, dst_ref=dst, send_sem=send.at[at], recv_sem=recv.at[at], device_id=device, device_id_type=MESH
        )

    def send(self, key, src, dst, device):
        copy = self.copy(key, src, dst, device)
        copy.start()
        self.sent.append(copy)

    def wait(self, key, ref, device):
        self.copy(key, ref, ref, device).wait_recv()

    def finish(self):
        for copy in self.sent:
            copy.wait_send()


def kernel(
    traj, noise, shift, scale, size, table, pmap, wq, wo, out,
    stage, shard, slots, perm, w, wt, mod, sizes, q, k, v, own_t, parts, sums, before, give, full, send, recv,
):
    seg, step = lax.axis_index("seg"), lax.axis_index("step")
    x, y, core, z = lax.rem(seg, XN), lax.div(seg, XN), lax.rem(step, 2), lax.div(step, 2)
    net = Net(send, recv)

    def ring(i, n):
        return lax.rem(i + n, n)

    def seg_of(dx, dy):
        return ring(y + dy, YN) * XN + ring(x + dx, XN)

    def at_seg(dx, dy):
        return (seg_of(dx, dy), step)

    def at_z(dz):
        return (seg, ring(z + dz, ZN) * 2 + core)

    sibling = (seg, z * 2 + 1 - core)
    following, preceding = (ring(seg + 1, SEGS), step), (ring(seg - 1, SEGS), step)

    peers = [(seg, ring(step + i, STEPS)) for i in range(1, STEPS)]
    peers += [at_seg(i, 0) for i in range(1, XN)] + [at_seg(0, 1), at_seg(0, -1), following, preceding]
    barrier = pltpu.get_barrier_semaphore()
    for peer in peers:
        pl.semaphore_signal(barrier, inc=1, device_id=peer, device_id_type=MESH)

    rows = wq[...].astype(F32)
    stage[...] = jnp.zeros_like(stage)
    for half in range(2):
        for c in range(CHUNKS):
            col = ((c // 3) * 6 + half * 3 + c % 3) * 128
            stage[half, c * SHARD : (c + 1) * SHARD, :] = rows[:, col : col + 128]
    shard[...] = stage[...].astype(BF16)
    pl.semaphore_wait(barrier, len(peers))

    for dz in range(ZN):
        for other in range(2):
            if (dz, other) == (0, 0):
                continue
            there = lax.rem(core + other, 2)
            net.send(
                ("z", dz, other), shard.at[there], slots.at[step], (seg, ring(z + dz, ZN) * 2 + there)
            )
    slots[step] = shard[core]

    onehot = (lax.broadcasted_iota(jnp.int32, (8, ROWS), 0) == pmap[...]).astype(F32)
    chosen = dot(onehot, table[...], ((0,), (0,)), lax.Precision.HIGHEST)
    inputs = traj[0].astype(F32) + chosen
    center = jnp.mean(inputs, axis=-1, keepdims=True)
    inputs = inputs - center
    spread = jnp.mean(jnp.square(inputs), axis=-1, keepdims=True)
    normed = inputs * lax.rsqrt(spread + 1e-06)
    mod[core, HALO : HALO + ROWS, :] = (normed * (1.0 + scale[...]) + shift[...]).astype(BF16)
    sizes[core] = jnp.full((8, 128), size[0], F32)

    mine, low, high = (slice(HALO, HALO + ROWS), slice(HALO, 2 * HALO), slice(ROWS, ROWS + HALO))
    first, last = slice(0, HALO), slice(HALO + ROWS, KEYS)
    net.send("up", mod.at[core, high], mod.at[core, first], following)
    net.send("down", mod.at[core, low], mod.at[core, last], preceding)
    net.send("own", mod.at[core, mine], mod.at[core, mine], sibling)
    net.send("size", sizes.at[core], sizes.at[core], sibling)

    shape = (BLOCK, STEPS * SLOT)
    i = lax.broadcasted_iota(jnp.int32, shape, 0)
    third = lax.shift_right_logical(i * 43, 7)
    j = lax.broadcasted_iota(jnp.int32, shape, 1) - third * SLOT - (i - third * SHARD)
    for c in range(CHUNKS):
        perm[c * BLOCK : (c + 1) * BLOCK, :] = jnp.where(j == c * SHARD, 1.0, 0.0).astype(BF16)
    for dz in range(ZN):
        for other in range(2):
            if (dz, other) == (0, 0):
                continue
            source = ring(z - dz, ZN) * 2 + lax.rem(core + other, 2)
            net.wait(("z", dz, other), slots.at[source], sibling)
    block = dot(perm[...], slots[...].reshape(STEPS * SLOT, 128)).astype(BF16)

    def w_rows(dx, dy):
        return pl.ds(pl.multiple_of(seg_of(dx, dy) * BLOCK, BLOCK), BLOCK)

    for c in range(CHUNKS):
        w[w_rows(0, 0), c * 128 : (c + 1) * 128] = block[c * BLOCK : (c + 1) * BLOCK]

    def part_a(dx, dy):
        return w.at[w_rows(dx, dy), 0:CUT]

    def part_b(dx, dy):
        return w.at[w_rows(dx, dy), CUT : CHUNKS * 128]

    def send_ax(dx, way):
        net.send(("ax", (dx - way) % XN), part_a(dx, 0), part_a(dx, 0), at_seg(way, 0))

    def wait_ax(dx):
        net.wait(("ax", dx % XN), part_a(dx, 0), sibling)

    def goes(way, far, is_b, dx=0):
        if far < YN // 2:
            return True
        return far == YN // 2 and (way == 1) == (is_b or dx == 0)

    def send_ay(dx, way, far):
        if goes(way, far + 1, False, dx):
            ref = part_a(dx, -way * far)
            net.send(("ay", dx, way, far + 1), ref, ref, at_seg(0, way))

    def wait_ay(dx, way, far):
        net.wait(("ay", dx, way, far), part_a(dx, -way * far), sibling)

    def send_by(way, far):
        if goes(way, far + 1, True):
            ref = part_b(0, -way * far)
            net.send(("by", way, far + 1), ref, ref, at_seg(0, way))

    def wait_by(way, far):
        net.wait(("by", way, far), part_b(0, -way * far), sibling)

    def send_bx(dx, dy, way):
        ref = part_b(dx, dy)
        net.send(("bx", dy, (dx - way) % XN), ref, ref, at_seg(way, 0))

    def wait_bx(dx, dy):
        net.wait(("bx", dy, dx % XN), part_b(dx, dy), sibling)

    def relay_bx(dy, way):
        wait_bx(-way, dy)
        send_bx(-way, dy, way)

    def wt_rows(dz, c):
        return wt.at[pl.ds(pl.multiple_of((ring(z + dz, ZN) * 2 + c) * WO, WO), WO)]

    def send_wz(way, far):
        if far + 1 < ZN // 2 or (far + 1 == ZN // 2 and way == 1):
            ref = wt_rows(-way * far, core)
            net.send(("wz", way, far + 1), ref, ref, at_z(way))

    def take_wz(way, far):
        ref = wt_rows(-way * far, core)
        net.wait(("wz", way, far), ref, sibling)
        send_wz(way, far)
        net.send(("ws", way, far), ref, ref, sibling)

    def wait_ws(way, far):
        net.wait(("ws", way, far), wt_rows(-way * far, 1 - core), sibling)

    send_ax(0, 1)
    send_ax(0, -1)
    send_by(1, 0)
    send_by(-1, 0)
    send_ay(0, 1, 0)
    send_ay(0, -1, 0)
    send_bx(0, 0, 1)
    send_bx(0, 0, -1)

    wt[pl.ds(pl.multiple_of(step * WO, WO), WO), :] = wo[...].T
    send_wz(1, 0)
    send_wz(-1, 0)
    net.send(("ws", 1, 0), wt_rows(0, core), wt_rows(0, core), sibling)

    wait_ax(-1)
    send_ax(-1, 1)
    send_ay(-1 % XN, 1, 0)
    send_ay(-1 % XN, -1, 0)
    wait_ax(1)
    send_ay(1, 1, 0)
    send_ay(1, -1, 0)
    wait_ax(2)
    send_ay(2, 1, 0)
    send_ay(2, -1, 0)
    relay_bx(0, 1)
    net.wait("up", mod.at[core, first], sibling)
    net.send("ups", mod.at[core, first], mod.at[core, first], sibling)
    net.wait("down", mod.at[core, last], sibling)
    net.send("downs", mod.at[core, last], mod.at[core, last], sibling)

    for far in range(1, YN // 2 + 1):
        for way in (1, -1):
            if goes(way, far, True):
                wait_by(way, far)
                send_by(way, far)
                send_bx(0, -way * far, 1)
                send_bx(0, -way * far, -1)
            for dx in (0, 3, 1, 2):
                if goes(way, far, False, dx):
                    wait_ay(dx, way, far)
                    send_ay(dx, way, far)
        for way in (1, -1):
            if far < ZN // 2 or way == 1:
                take_wz(way, far)
        for way in (1, -1):
            if goes(way, far, True):
                relay_bx(-way * far, way)
    for dy in range(-(YN // 2), YN // 2):
        way = -1 if dy > 0 else 1
        wait_bx(way, dy)
        wait_bx(2, dy)
    other = 1 - core
    net.wait("own", mod.at[other, mine], sibling)
    net.wait("ups", mod.at[other, first], sibling)
    net.wait("downs", mod.at[other, last], sibling)
    net.wait("size", sizes.at[other], sibling)

    for c in range(3):
        cols = slice(c * 128, (c + 1) * 128)
        k_cols = slice(HALF + c * 128, HALF + (c + 1) * 128)
        v_cols = slice(2 * HALF + c * 128, 2 * HALF + (c + 1) * 128)
        everyone = mod[...].reshape(2 * KEYS, D)
        asked = mod[:, mine, :].reshape(2 * ROWS, D)
        q[c] = (dot(asked, w[:, cols]).astype(BF16) * 0.125).astype(BF16).reshape(2, ROWS, 128)
        k[c] = dot(everyone, w[:, k_cols]).astype(BF16).reshape(2, KEYS, 128)
        v[c] = dot(everyone, w[:, v_cols]).astype(BF16).reshape(2, KEYS, 128)

    at_q = lax.broadcasted_iota(jnp.int32, (ROWS, KEYS), 0)
    at_k = lax.broadcasted_iota(jnp.int32, (ROWS, KEYS), 1)
    frame = seg * ROWS - HALO + at_k
    allowed = (at_k >= at_q) & (at_k <= at_q + 2 * HALO) & (frame >= 0) & (frame < SEGS * ROWS)
    bias = jnp.where(allowed, 0.0, -1e30).astype(F32)
    bias = jnp.concatenate([bias, bias], axis=0)
    lane = lax.broadcasted_iota(jnp.int32, (ROWS, 128), 1)
    ones = jnp.ones((KEYS, 128), BF16)
    for c in range(3):
        total = None
        for s in range(2):
            asked = q[c, s]
            nothing = jnp.zeros_like(asked)
            both = jnp.concatenate([jnp.where(lane < 64, asked, nothing), jnp.where(lane < 64, nothing, asked)], axis=0)
            scores = dot(both, k[c, s], ((1,), (1,))) + bias
            lifted = jnp.exp(scores - jnp.max(scores, axis=1, keepdims=True)).astype(BF16)
            got = dot(lifted, v[c, s]) / dot(lifted, ones)
            got = jnp.where(lane < 64, got[:ROWS], got[ROWS:]).astype(BF16)
            term = got.astype(F32) * sizes[s, 0:1, :]
            if s == 0:
                own_t[:, c * 128 : (c + 1) * 128] = term.astype(BF16)
                total = term
            else:
                total = total + term
        give[:, c * 128 : (c + 1) * 128] = total.astype(BF16)

    part = ROWS // ZN

    def part_rows(i):
        return pl.ds(pl.multiple_of(i * part, part), part)

    for dz in range(1, ZN):
        net.send(("there", dz), give.at[part_rows(ring(z + dz, ZN))], parts.at[z], at_z(dz))
    parts[z] = give[part_rows(z), :]
    for dz in range(1, ZN):
        net.wait(("there", dz), parts.at[ring(z - dz, ZN)], sibling)
    total = jnp.zeros((part, HALF), F32)
    for i in range(ZN):
        sums[i] = total.astype(BF16)
        total = total + parts[i].astype(F32)
    for dz in range(1, ZN):
        net.send(("back", dz), sums.at[ring(z + dz, ZN)], before.at[part_rows(z)], at_z(dz))
    before[part_rows(z), :] = sums[z]
    for dz in range(1, ZN):
        net.wait(("back", dz), before.at[part_rows(ring(z - dz, ZN))], sibling)

    even = before[...]
    odd = (even.astype(F32) + own_t[...].astype(F32)).astype(BF16)
    full[core] = jnp.where(core == 0, even, odd)
    sums_there = jnp.where(core == 0, odd, even)
    own_t[...] = sums_there
    net.send("full", own_t, full.at[core], sibling)
    for far in range(0, ZN // 2 + 1):
        for way in (1, -1):
            if (far > 0 or way == 1) and (far < ZN // 2 or way == 1):
                wait_ws(way, far)
    net.wait("full", full.at[other], sibling)
    drift = dot(full[0], wt[:, 0:HALF], ((1,), (1,))) + dot(full[1], wt[:, HALF:HQ], ((1,), (1,)))
    out[...] = (noise[...].astype(F32) + drift).astype(BF16)
    net.finish()


def shards(trajectory, noise, mod_shift, mod_scale, step_size, prompt_table, prompt_map, w_qkv, w_out):
    vmem = pl.BlockSpec(memory_space=pltpu.VMEM)
    smem = pl.BlockSpec(memory_space=pltpu.SMEM)
    result = pl.pallas_call(
        kernel,
        out_shape=jax.ShapeDtypeStruct((ROWS, D), BF16),
        in_specs=[vmem, vmem, vmem, vmem, smem, vmem, vmem, vmem, vmem],
        out_specs=vmem,
        scratch_shapes=[
            pltpu.VMEM((2, SLOT, 128), F32),
            pltpu.VMEM((2, SLOT, 128), BF16),
            pltpu.VMEM((STEPS, SLOT, 128), BF16),
            pltpu.VMEM((CHUNKS * BLOCK, STEPS * SLOT), BF16),
            pltpu.VMEM((D, CHUNKS * 128), BF16),
            pltpu.VMEM((D, HQ), BF16),
            pltpu.VMEM((2, KEYS, D), BF16),
            pltpu.VMEM((2, 8, 128), F32),
            pltpu.VMEM((3, 2, ROWS, 128), BF16),
            pltpu.VMEM((3, 2, KEYS, 128), BF16),
            pltpu.VMEM((3, 2, KEYS, 128), BF16),
            pltpu.VMEM((ROWS, HALF), BF16),
            pltpu.VMEM((ZN, ROWS // ZN, HALF), BF16),
            pltpu.VMEM((ZN, ROWS // ZN, HALF), BF16),
            pltpu.VMEM((ROWS, HALF), BF16),
            pltpu.VMEM((ROWS, HALF), BF16),
            pltpu.VMEM((2, ROWS, HALF), BF16),
            pltpu.SemaphoreType.DMA((SEMS,)),
            pltpu.SemaphoreType.DMA((SEMS,)),
        ],
        compiler_params=pltpu.CompilerParams(
            collective_id=0, has_side_effects=True, vmem_limit_bytes=48 * 1024 * 1024
        ),
    )(
        trajectory, noise, mod_shift, mod_scale, step_size, prompt_table,
        prompt_map.reshape(1, ROWS), w_qkv, w_out,
    )
    return result[None]


def solution(mesh):
    return jax.shard_map(
        shards,
        mesh=mesh,
        in_specs=(
            P("step", "seg", None),
            P("seg", None),
            P("step", None),
            P("step", None),
            P("step"),
            P(),
            P("seg"),
            P(("seg", "step"), None),
            P(None, "step"),
        ),
        out_specs=P("step", "seg", None),
        check_vma=False,
    )
```

```python
import functools

import jax
import jax.numpy as jnp
from jax import lax
from jax.experimental import pallas as pl
from jax.experimental.pallas import tpu as pltpu
from jax.sharding import PartitionSpec as P

MESH = pl.DeviceIdType.MESH
BF16 = jnp.bfloat16
F32 = jnp.float32
XN, YN, ZN = 4, 8, 8
SEGS, STEPS = XN * YN, 2 * ZN
ROWS, HALO, D, HQ = 128, 64, 1536, 768
KEYS = ROWS + 2 * HALO
HALF = HQ // 2
CHUNKS = 9
SHARD = 3
BLOCK = SHARD * STEPS
SLOT = 32
WO = D // STEPS
PAIR = 2 * XN * BLOCK
SEMS = 160


def dot(a, b, contract=((1,), (0,)), precision=None):
    return lax.dot_general(a, b, (contract, ((), ())), preferred_element_type=F32, precision=precision)


class Net:
    def __init__(self, send, recv):
        self.sems, self.index, self.sent = (send, recv), {}, []

    def copy(self, key, src, dst, device):
        at = self.index.setdefault(key, len(self.index))
        send, recv = self.sems
        return pltpu.make_async_remote_copy(
            src_ref=src, dst_ref=dst, send_sem=send.at[at], recv_sem=recv.at[at], device_id=device, device_id_type=MESH
        )

    def send(self, key, src, dst, device):
        copy = self.copy(key, src, dst, device)
        copy.start()
        self.sent.append(copy)

    def wait(self, key, ref, device):
        self.copy(key, ref, ref, device).wait_recv()

    def finish(self):
        for copy in self.sent:
            copy.wait_send()


def kernel(
    traj_hbm, noise_hbm, shift_hbm, scale_hbm, size, table_hbm, pmap_hbm, wq_hbm, wo_hbm, out,
    traj, noise, shift, scale, table, pmap, wq, stage, shard, slots, perm, w, wt, mod, sizes,
    sum_q, sum_kv, q, k, v, own_t, parts, sums, before, give, full, load, send, recv,
):
    seg, step = lax.axis_index("seg"), lax.axis_index("step")
    x, y, core, z = lax.rem(seg, XN), lax.div(seg, XN), lax.rem(step, 2), lax.div(step, 2)
    other = 1 - core
    net = Net(send, recv)

    def ring(i, n):
        return lax.rem(i + n, n)

    def seg_of(dx, dy):
        return ring(y + dy, YN) * XN + ring(x + dx, XN)

    def at_seg(dx, dy):
        return (seg_of(dx, dy), step)

    def at_z(dz):
        return (seg, ring(z + dz, ZN) * 2 + core)

    sibling = (seg, z * 2 + other)
    following, preceding = (ring(seg + 1, SEGS), step), (ring(seg - 1, SEGS), step)

    peers = [(seg, ring(step + i, STEPS)) for i in range(1, STEPS)]
    peers += [at_seg(i, 0) for i in range(1, XN)] + [at_seg(0, 1), at_seg(0, -1), following, preceding]
    barrier = pltpu.get_barrier_semaphore()
    for peer in peers:
        pl.semaphore_signal(barrier, inc=1, device_id=peer, device_id_type=MESH)

    def wt_rows(dz, c):
        return wt.at[pl.ds(pl.multiple_of((ring(z + dz, ZN) * 2 + c) * WO, WO), WO)]

    loads = [
        pltpu.make_async_copy(src, dst, load.at[i])
        for i, (src, dst) in enumerate(
            [
                (wq_hbm, wq), (traj_hbm, traj), (pmap_hbm, pmap), (table_hbm, table), (shift_hbm, shift),
                (scale_hbm, scale), (wo_hbm, wt_rows(0, core)), (noise_hbm, noise),
            ]
        )
    ]
    for copy in loads:
        copy.start()

    stage[...] = jnp.zeros_like(stage)
    loads[0].wait()
    rows = wq[...].astype(F32)
    for half in range(2):
        for c in range(CHUNKS):
            col = ((c // 3) * 6 + half * 3 + c % 3) * 128
            stage[half, c * SHARD : (c + 1) * SHARD, :] = rows[:, col : col + 128]
    shard[...] = stage[...].astype(BF16)
    slots[step] = shard[core]
    pl.semaphore_wait(barrier, len(peers))

    for dz in (4, 3, 5, 2, 6, 1, 7, 0):
        for swap in range(2):
            if (dz, swap) == (0, 0):
                continue
            there = lax.rem(core + swap, 2)
            net.send(("z", dz, swap), shard.at[there], slots.at[step], (seg, ring(z + dz, ZN) * 2 + there))

    shape = (BLOCK, STEPS * SLOT)
    i = lax.broadcasted_iota(jnp.int32, shape, 0)
    third = lax.shift_right_logical(i * 43, 7)
    j = lax.broadcasted_iota(jnp.int32, shape, 1) - third * SLOT - (i - third * SHARD)
    for c in range(CHUNKS):
        perm[c * BLOCK : (c + 1) * BLOCK, :] = jnp.where(j == c * SHARD, 1.0, 0.0).astype(BF16)
    for dz in range(ZN):
        for swap in range(2):
            if (dz, swap) == (0, 0):
                continue
            source = ring(z - dz, ZN) * 2 + lax.rem(core + swap, 2)
            net.wait(("z", dz, swap), slots.at[source], sibling)
    block = dot(perm[...], slots[...].reshape(STEPS * SLOT, 128)).astype(BF16)

    ours = 1 + lax.rem(z, 2)

    def part(which, dx, dy):
        return w.at[which, pl.ds(pl.multiple_of(seg_of(dx, dy) * BLOCK, BLOCK), BLOCK)]

    for c in range(CHUNKS):
        own_rows = pl.ds(pl.multiple_of(seg * BLOCK, BLOCK), BLOCK)
        w[c // 3, own_rows, (c % 3) * 128 : (c % 3 + 1) * 128] = block[c * BLOCK : (c + 1) * BLOCK]

    def goes(way, far, is_b, dx=0):
        if far < YN // 2:
            return True
        return far == YN // 2 and (way == 1) == (is_b or dx % 2 == 0)

    def send_ax(dx, way):
        ref = part(ours, dx, 0)
        net.send(("ax", (dx - way) % XN), ref, ref, at_seg(way, 0))

    def wait_ax(dx):
        net.wait(("ax", dx % XN), part(ours, dx, 0), sibling)

    def send_ay(dx, way, far):
        if goes(way, far + 1, False, dx):
            ref = part(ours, dx, -way * far)
            net.send(("ay", dx, way, far + 1), ref, ref, at_seg(0, way))

    def wait_ay(dx, way, far):
        net.wait(("ay", dx, way, far), part(ours, dx, -way * far), sibling)

    def send_az(dx, dy):
        ref = part(ours, dx, dy)
        net.send(("az", dx, dy % YN), ref, ref, at_z(1 if dx % 2 == 0 else -1))

    def wait_az(dx, dy):
        net.wait(("az", dx, dy % YN), part(3 - ours, dx, dy), sibling)

    def send_by(way, far):
        if goes(way, far + 1, True):
            ref = part(0, 0, -way * far)
            net.send(("by", way, far + 1), ref, ref, at_seg(0, way))

    def wait_by(way, far):
        net.wait(("by", way, far), part(0, 0, -way * far), sibling)

    def send_bx(dx, dy, way):
        ref = part(0, dx, dy)
        net.send(("bx", dy, (dx - way) % XN), ref, ref, at_seg(way, 0))

    def wait_bx(dx, dy):
        net.wait(("bx", dy, dx % XN), part(0, dx, dy), sibling)

    def relay_bx(dy, way):
        wait_bx(-way, dy)
        send_bx(-way, dy, way)

    def send_wz(way, far):
        if far + 1 < ZN // 2 or (far + 1 == ZN // 2 and way == 1):
            ref = wt_rows(-way * far, core)
            net.send(("wz", way, far + 1), ref, ref, at_z(way))

    def take_wz(way, far):
        if far < ZN // 2 or way == 1:
            ref = wt_rows(-way * far, core)
            net.wait(("wz", way, far), ref, sibling)
            send_wz(way, far)
            net.send(("ws", way, far), ref, ref, sibling)

    def wait_ws(way, far):
        if (far > 0 or way == 1) and (far < ZN // 2 or way == 1):
            net.wait(("ws", way, far), wt_rows(-way * far, 1 - core), sibling)

    mine, low, high = (slice(HALO, HALO + ROWS), slice(HALO, 2 * HALO), slice(ROWS, ROWS + HALO))
    first, last = slice(0, HALO), slice(HALO + ROWS, KEYS)

    def project(pair, start):
        rows = pl.ds(pl.multiple_of(pair * PAIR, PAIR), PAIR)
        everyone = mod[:, :, rows].reshape(2 * KEYS, PAIR)
        asked = mod[:, mine, rows].reshape(2 * ROWS, PAIR)
        add_q, add_k, add_v = dot(asked, w[0, rows]), dot(everyone, w[1, rows]), dot(everyone, w[2, rows])
        sum_q[...] = add_q if start else sum_q[...] + add_q
        sum_kv[0] = add_k if start else sum_kv[0] + add_k
        sum_kv[1] = add_v if start else sum_kv[1] + add_v

    send_ax(0, 1)
    send_ax(0, -1)
    send_ay(0, 1, 0)
    send_ay(0, -1, 0)
    net.send(("ax", 2), part(ours, 0, 0), part(ours, 0, 0), at_seg(2, 0))
    send_by(1, 0)
    send_by(-1, 0)
    send_bx(0, 0, 1)
    send_bx(0, 0, -1)

    for copy in loads[1:]:
        copy.wait()
    onehot = (lax.broadcasted_iota(jnp.int32, (8, ROWS), 0) == pmap[...]).astype(F32)
    chosen = dot(onehot, table[...], ((0,), (0,)), lax.Precision.HIGHEST)
    inputs = traj[0].astype(F32) + chosen
    center = jnp.mean(inputs, axis=-1, keepdims=True)
    inputs = inputs - center
    spread = jnp.mean(jnp.square(inputs), axis=-1, keepdims=True)
    normed = inputs * lax.rsqrt(spread + 1e-06)
    mod[core, mine, :] = (normed * (1.0 + scale[...]) + shift[...]).astype(BF16)
    sizes[core] = jnp.full((8, 128), size[0], F32)

    for dx in (3, 1, 2):
        wait_ax(dx)
        send_ay(dx, 1, 0)
        send_ay(dx, -1, 0)
        send_az(dx, 0)
    net.send("up", mod.at[core, high], mod.at[core, first], following)
    net.send("down", mod.at[core, low], mod.at[core, last], preceding)
    net.send("own", mod.at[core, mine], mod.at[core, mine], sibling)
    net.send("size", sizes.at[core], sizes.at[core], sibling)
    relay_bx(0, 1)

    last_level = YN // 2
    pair = lax.div(y, 2)
    side = 1 - 2 * lax.rem(y, 2)
    pairs = [pair, ring(pair - side, YN // 2), ring(pair + side, YN // 2), ring(pair + 2, YN // 2)]

    def settle(far):
        for dy in {far % YN, -far % YN}:
            dy = dy - YN if dy >= YN // 2 else dy
            wait_bx(-1 if dy > 0 else 1, dy)
            if abs(dy) == last_level:
                wait_bx(-1, dy)
            wait_bx(2, dy)
            for dx in range(XN):
                if (dx, dy) != (0, 0):
                    wait_az(dx, dy)

    for far in range(1, last_level + 1):
        for way in (1, -1):
            if goes(way, far, True):
                wait_by(way, far)
                send_by(way, far)
                send_bx(0, -way * far, 1)
                send_bx(0, -way * far, -1)
                if far == last_level:
                    ref = part(0, 0, -way * far)
                    net.send(("bx", -way * far, 2), ref, ref, at_seg(2, 0))
        for dx in (0, 3, 1, 2):
            for way in (1, -1):
                if goes(way, far, False, dx):
                    wait_ay(dx, way, far)
                    send_ay(dx, way, far)
                    send_az(dx, -way * far)
        for way in (1, -1):
            if goes(way, far, True) and far < last_level:
                relay_bx(-way * far, way)
        if far == 1:
            net.wait("up", mod.at[core, first], sibling)
            net.send("ups", mod.at[core, first], mod.at[core, first], sibling)
            net.wait("down", mod.at[core, last], sibling)
            net.send("downs", mod.at[core, last], mod.at[core, last], sibling)
            settle(0)
        if far == 2:
            net.wait("own", mod.at[other, mine], sibling)
            net.wait("ups", mod.at[other, first], sibling)
            net.wait("downs", mod.at[other, last], sibling)
            net.wait("size", sizes.at[other], sibling)
        if far > 1:
            settle(far - 1)
            project(pairs[far - 2], far == 2)
    send_wz(1, 0)
    send_wz(-1, 0)
    net.send(("ws", 1, 0), wt_rows(0, core), wt_rows(0, core), sibling)
    settle(last_level)
    project(pairs[3], False)
    take_wz(1, 1)
    take_wz(-1, 1)
    for c in range(3):
        cols = slice(c * 128, (c + 1) * 128)
        q[c] = (sum_q[:, cols].astype(BF16) * 0.125).astype(BF16).reshape(2, ROWS, 128)
        k[c] = sum_kv[0, :, cols].astype(BF16).reshape(2, KEYS, 128)
        v[c] = sum_kv[1, :, cols].astype(BF16).reshape(2, KEYS, 128)

    at_q = lax.broadcasted_iota(jnp.int32, (ROWS, KEYS), 0)
    at_k = lax.broadcasted_iota(jnp.int32, (ROWS, KEYS), 1)
    frame = seg * ROWS - HALO + at_k
    allowed = (at_k >= at_q) & (at_k <= at_q + 2 * HALO) & (frame >= 0) & (frame < SEGS * ROWS)
    bias = jnp.where(allowed, 0.0, -1e30).astype(F32)
    bias = jnp.concatenate([bias, bias], axis=0)
    lane = lax.broadcasted_iota(jnp.int32, (ROWS, 128), 1)
    ones = jnp.ones((KEYS, 128), BF16)
    for c in range(3):
        total = None
        for s in range(2):
            asked = q[c, s]
            nothing = jnp.zeros_like(asked)
            both = jnp.concatenate([jnp.where(lane < 64, asked, nothing), jnp.where(lane < 64, nothing, asked)], axis=0)
            scores = dot(both, k[c, s], ((1,), (1,))) + bias
            lifted = jnp.exp(scores - jnp.max(scores, axis=1, keepdims=True)).astype(BF16)
            got = dot(lifted, v[c, s]) / dot(lifted, ones)
            got = jnp.where(lane < 64, got[:ROWS], got[ROWS:]).astype(BF16)
            term = got.astype(F32) * sizes[s, 0:1, :]
            if s == 0:
                own_t[:, c * 128 : (c + 1) * 128] = term.astype(BF16)
                total = term
            else:
                total = total + term
        give[:, c * 128 : (c + 1) * 128] = total.astype(BF16)
        if c == 1:
            take_wz(1, 2)
            take_wz(-1, 2)

    share = ROWS // ZN

    def share_rows(i):
        return pl.ds(pl.multiple_of(i * share, share), share)

    for dz in (4, 3, 5, 2, 6, 1, 7):
        net.send(("there", dz), give.at[share_rows(ring(z + dz, ZN))], parts.at[z], at_z(dz))
    parts[z] = give[share_rows(z), :]
    take_wz(1, 3)
    take_wz(-1, 3)
    for dz in range(1, ZN):
        net.wait(("there", dz), parts.at[ring(z - dz, ZN)], sibling)
    total = jnp.zeros((share, HALF), F32)
    for i in range(ZN):
        sums[i] = total.astype(BF16)
        total = total + parts[i].astype(F32)
    for dz in (4, 3, 5, 2, 6, 1, 7):
        net.send(("back", dz), sums.at[ring(z + dz, ZN)], before.at[share_rows(z)], at_z(dz))
    before[share_rows(z), :] = sums[z]
    take_wz(1, 4)
    for dz in range(1, ZN):
        net.wait(("back", dz), before.at[share_rows(ring(z - dz, ZN))], sibling)

    even = before[...]
    odd = (even.astype(F32) + own_t[...].astype(F32)).astype(BF16)
    full[core] = jnp.where(core == 0, even, odd)
    own_t[...] = jnp.where(core == 0, odd, even)
    net.send("full", own_t, full.at[core], sibling)
    for far in range(0, ZN // 2 + 1):
        wait_ws(1, far)
        wait_ws(-1, far)
    net.wait("full", full.at[other], sibling)
    drift = dot(full[0], wt[:, 0:HALF], ((1,), (1,))) + dot(full[1], wt[:, HALF:HQ], ((1,), (1,)))
    out[...] = (noise[...].astype(F32) + drift).astype(BF16)
    net.finish()


def shards(trajectory, noise, mod_shift, mod_scale, step_size, prompt_table, prompt_map, w_qkv, w_out):
    vmem = pl.BlockSpec(memory_space=pltpu.VMEM)
    smem = pl.BlockSpec(memory_space=pltpu.SMEM)
    hbm = pl.BlockSpec(memory_space=pl.ANY)
    result = pl.pallas_call(
        kernel,
        out_shape=jax.ShapeDtypeStruct((ROWS, D), BF16),
        in_specs=[hbm, hbm, hbm, hbm, smem, hbm, hbm, hbm, hbm],
        out_specs=vmem,
        scratch_shapes=[
            pltpu.VMEM((1, ROWS, D), BF16),
            pltpu.VMEM((ROWS, D), BF16),
            pltpu.VMEM((1, D), F32),
            pltpu.VMEM((1, D), F32),
            pltpu.VMEM((8, D), F32),
            pltpu.VMEM((1, ROWS), jnp.int32),
            pltpu.VMEM((SHARD, 3 * HQ), BF16),
            pltpu.VMEM((2, SLOT, 128), F32),
            pltpu.VMEM((2, SLOT, 128), BF16),
            pltpu.VMEM((STEPS, SLOT, 128), BF16),
            pltpu.VMEM((CHUNKS * BLOCK, STEPS * SLOT), BF16),
            pltpu.VMEM((3, D, HALF), BF16),
            pltpu.VMEM((D, HQ), BF16),
            pltpu.VMEM((2, KEYS, D), BF16),
            pltpu.VMEM((2, 8, 128), F32),
            pltpu.VMEM((2 * ROWS, HALF), F32),
            pltpu.VMEM((2, 2 * KEYS, HALF), F32),
            pltpu.VMEM((3, 2, ROWS, 128), BF16),
            pltpu.VMEM((3, 2, KEYS, 128), BF16),
            pltpu.VMEM((3, 2, KEYS, 128), BF16),
            pltpu.VMEM((ROWS, HALF), BF16),
            pltpu.VMEM((ZN, ROWS // ZN, HALF), BF16),
            pltpu.VMEM((ZN, ROWS // ZN, HALF), BF16),
            pltpu.VMEM((ROWS, HALF), BF16),
            pltpu.VMEM((ROWS, HALF), BF16),
            pltpu.VMEM((2, ROWS, HALF), BF16),
            pltpu.SemaphoreType.DMA((8,)),
            pltpu.SemaphoreType.DMA((SEMS,)),
            pltpu.SemaphoreType.DMA((SEMS,)),
        ],
        compiler_params=pltpu.CompilerParams(
            collective_id=0, has_side_effects=True, vmem_limit_bytes=60 * 1024 * 1024
        ),
    )(
        trajectory, noise, mod_shift, mod_scale, step_size, prompt_table,
        prompt_map.reshape(1, ROWS), w_qkv, w_out.T,
    )
    return result[None]


def solution(mesh):
    return jax.shard_map(
        shards,
        mesh=mesh,
        in_specs=(
            P("step", "seg", None),
            P("seg", None),
            P("step", None),
            P("step", None),
            P("step"),
            P(),
            P("seg"),
            P(("seg", "step"), None),
            P(None, "step"),
        ),
        out_specs=P("step", "seg", None),
        check_vma=False,
    )
```

```python
import functools

import jax
import jax.numpy as jnp
from jax import lax
from jax.experimental import pallas as pl
from jax.experimental.pallas import tpu as pltpu
from jax.sharding import PartitionSpec as P

MESH = pl.DeviceIdType.MESH
BF16 = jnp.bfloat16
F32 = jnp.float32
XN, YN, ZN = 4, 8, 8
SEGS, STEPS = XN * YN, 2 * ZN
ROWS, HALO, D, HQ = 128, 64, 1536, 768
KEYS = ROWS + 2 * HALO
HALF = HQ // 2
CHUNKS = 9
SHARD = 3
BLOCK = SHARD * STEPS
SLOT = 32
WO = D // STEPS
PAIR = 2 * XN * BLOCK
SENDS, RECVS = 12, 80


def dot(a, b, contract=((1,), (0,)), precision=None):
    return lax.dot_general(a, b, (contract, ((), ())), preferred_element_type=F32, precision=precision)


class Net:
    def __init__(self, send, recv):
        self.sems, self.index, self.count = (send, recv), ({}, {}), {}

    def sem(self, side, name):
        index = self.index[side]
        return self.sems[side].at[index.setdefault(name, len(index))]

    def send(self, group, name, src, dst, device):
        self.count[group] = self.count.get(group, 0) + 1
        pltpu.make_async_remote_copy(
            src_ref=src, dst_ref=dst, send_sem=self.sem(0, group), recv_sem=self.sem(1, name),
            device_id=device, device_id_type=MESH,
        ).start()

    def wait(self, name, ref, device):
        pltpu.make_async_remote_copy(
            src_ref=ref, dst_ref=ref, send_sem=self.sems[0].at[0], recv_sem=self.sem(1, name),
            device_id=device, device_id_type=MESH,
        ).wait_recv()

    def sent(self, group, ref, device):
        pltpu.make_async_remote_copy(
            src_ref=ref, dst_ref=ref, send_sem=self.sem(0, group), recv_sem=self.sems[1].at[0],
            device_id=device, device_id_type=MESH,
        ).wait_send()


def kernel(
    traj_hbm, noise_hbm, shift_hbm, scale_hbm, size, table_hbm, pmap_hbm, wq_hbm, wo_hbm, out,
    traj, noise, shift, scale, table, pmap, wq, stage, shard, slots, perm, w, wt, mod, sizes,
    sum_q, sum_kv, q, k, v, own_t, parts, sums, before, give, full, load, send, recv,
):
    seg, step = lax.axis_index("seg"), lax.axis_index("step")
    x, y, core, z = lax.rem(seg, XN), lax.div(seg, XN), lax.rem(step, 2), lax.div(step, 2)
    other = 1 - core
    net = Net(send, recv)

    def ring(i, n):
        return lax.rem(i + n, n)

    def seg_of(dx, dy):
        return ring(y + dy, YN) * XN + ring(x + dx, XN)

    def at_seg(dx, dy):
        return (seg_of(dx, dy), step)

    def at_z(dz):
        return (seg, ring(z + dz, ZN) * 2 + core)

    sibling = (seg, z * 2 + other)
    following, preceding = (ring(seg + 1, SEGS), step), (ring(seg - 1, SEGS), step)

    peers = [(seg, ring(step + i, STEPS)) for i in range(1, STEPS)]
    peers += [at_seg(i, 0) for i in range(1, XN)] + [at_seg(0, i) for i in (1, -1, 2, -2)] + [following, preceding]
    barrier = pltpu.get_barrier_semaphore()
    for peer in peers:
        pl.semaphore_signal(barrier, inc=1, device_id=peer, device_id_type=MESH)

    near = lax.rem(x, 2)

    def wt_block(dz):
        return wt.at[near, ring(z + dz, ZN), core]

    sources = [
        (wq_hbm, wq), (traj_hbm, traj), (pmap_hbm, pmap), (table_hbm, table), (shift_hbm, shift), (scale_hbm, scale),
        (wo_hbm.at[:, pl.ds(pl.multiple_of(near * HALF, HALF), HALF)], wt_block(0)), (noise_hbm, noise),
    ]
    loads = [pltpu.make_async_copy(src, dst, load.at[i]) for i, (src, dst) in enumerate(sources)]
    for copy in loads:
        copy.start()

    stage[...] = jnp.zeros_like(stage)
    loads[0].wait()
    rows = wq[...].astype(F32)
    for half in range(2):
        for c in range(CHUNKS):
            col = ((c // 3) * 6 + half * 3 + c % 3) * 128
            stage[half, c * SHARD : (c + 1) * SHARD, :] = rows[:, col : col + 128]
    shard[...] = stage[...].astype(BF16)
    slots[step] = shard[core]
    pl.semaphore_wait(barrier, len(peers))

    for dz in (4, 3, 5, 2, 6, 1, 7, 0):
        for swap in range(2):
            if (dz, swap) == (0, 0):
                continue
            there = lax.rem(core + swap, 2)
            net.send("z", "z", shard.at[there], slots.at[step], (seg, ring(z + dz, ZN) * 2 + there))

    mine, low, high = (slice(HALO, HALO + ROWS), slice(HALO, 2 * HALO), slice(ROWS, ROWS + HALO))
    first, last = slice(0, HALO), slice(HALO + ROWS, KEYS)
    for copy in loads[1:]:
        copy.wait()
    onehot = (lax.broadcasted_iota(jnp.int32, (8, ROWS), 0) == pmap[...]).astype(F32)
    chosen = dot(onehot, table[...], ((0,), (0,)), lax.Precision.HIGHEST)
    inputs = traj[0].astype(F32) + chosen
    center = jnp.mean(inputs, axis=-1, keepdims=True)
    inputs = inputs - center
    spread = jnp.mean(jnp.square(inputs), axis=-1, keepdims=True)
    normed = inputs * lax.rsqrt(spread + 1e-06)
    mod[core, mine, :] = (normed * (1.0 + scale[...]) + shift[...]).astype(BF16)
    sizes[core] = jnp.full((8, 128), size[0], F32)
    net.send("mod", "up", mod.at[core, high], mod.at[core, first], following)
    net.send("mod", "down", mod.at[core, low], mod.at[core, last], preceding)
    net.send("mod", "mod", mod.at[core, mine], mod.at[core, mine], sibling)
    net.send("size", "size", sizes.at[core], sizes.at[core], sibling)

    shape = (BLOCK, STEPS * SLOT)
    i = lax.broadcasted_iota(jnp.int32, shape, 0)
    third = lax.shift_right_logical(i * 43, 7)
    j = lax.broadcasted_iota(jnp.int32, shape, 1) - third * SLOT - (i - third * SHARD)
    for c in range(CHUNKS):
        perm[c * BLOCK : (c + 1) * BLOCK, :] = jnp.where(j == c * SHARD, 1.0, 0.0).astype(BF16)
    net.wait("z", slots.at[0 : STEPS - 1], sibling)
    block = dot(perm[...], slots[...].reshape(STEPS * SLOT, 128)).astype(BF16)

    ours = 1 + lax.rem(z, 2)

    def part(which, dx, dy):
        return w.at[which, pl.ds(pl.multiple_of(seg_of(dx, dy) * BLOCK, BLOCK), BLOCK)]

    def blocks(n):
        return w.at[:, 0 : n * BLOCK // 3]

    for c in range(CHUNKS):
        own_rows = pl.ds(pl.multiple_of(seg * BLOCK, BLOCK), BLOCK)
        w[c // 3, own_rows, (c % 3) * 128 : (c % 3 + 1) * 128] = block[c * BLOCK : (c + 1) * BLOCK]

    def pass_on(name, ref, device):
        net.send("w", name, ref, ref, device)

    top = YN // 2

    def goes(way, far, is_b, dx=0):
        return far < top or (way == 1) == (is_b or dx % 2 == 0)

    def send_ax(way):
        pass_on(("ax", -way % XN), part(ours, 0, 0), at_seg(way, 0))

    def wait_ax(dx):
        net.wait(("ax", dx % XN), part(ours, dx, 0), sibling)

    def send_ay(dx, way, far):
        ref = part(ours, dx, -way * far)
        if far + 1 < top:
            pass_on(("ay", dx, way, far + 1), ref, at_seg(0, way))
        if far + 2 == top and goes(way, top, False, dx):
            pass_on(("ay", dx, way, top), ref, at_seg(0, 2 * way))

    def wait_ay(dx, way, far):
        net.wait(("ay", dx, way, far), part(ours, dx, -way * far), sibling)

    def send_az(dx, dy):
        pass_on(("az", abs(dy)), part(ours, dx, dy), at_z(1 if dx % 2 == 0 else -1))

    def send_by(way, far):
        ref = part(0, 0, -way * far)
        if far + 1 < top:
            pass_on(("by", way, far + 1), ref, at_seg(0, way))
        if far + 2 == top and goes(way, top, True):
            pass_on(("by", way, top), ref, at_seg(0, 2 * way))

    def wait_by(way, far):
        net.wait(("by", way, far), part(0, 0, -way * far), sibling)

    def relayed(far):
        return far < top - 1

    def send_bx(way_y, far):
        dy = -way_y * far
        relay = way_y if relayed(far) else 0
        for way in (1, -1):
            pass_on(("bxr", dy) if way == relay else ("bx", far), part(0, 0, dy), at_seg(way, 0))
        if not relay:
            pass_on(("bx", far), part(0, 0, dy), at_seg(2, 0))

    def relay_bx(way_y, far):
        dy = -way_y * far
        net.wait(("bxr", dy), part(0, -way_y, dy), sibling)
        pass_on(("bx", far), part(0, -way_y, dy), at_seg(way_y, 0))

    def settle(far):
        both = 2 if 0 < far < top else 1
        net.wait(("bx", far), blocks(both * (2 if relayed(far) else 3)), sibling)
        net.wait(("az", far), blocks(both * XN - (far == 0)), sibling)

    def send_wz(way, far):
        if far + 1 < ZN // 2 or (far + 1 == ZN // 2 and way == 1):
            net.send("wz", ("wz", way, far + 1), wt_block(-way * far), wt_block(-way * far), at_z(way))

    def take_wz(way, far):
        net.wait(("wz", way, far), wt_block(-way * far), sibling)
        send_wz(way, far)

    def project(pair, start):
        rows = pl.ds(pl.multiple_of(pair * PAIR, PAIR), PAIR)
        everyone = mod[:, :, rows].reshape(2 * KEYS, PAIR)
        asked = mod[:, mine, rows].reshape(2 * ROWS, PAIR)
        add_q, add_k, add_v = dot(asked, w[0, rows]), dot(everyone, w[1, rows]), dot(everyone, w[2, rows])
        sum_q[...] = add_q if start else sum_q[...] + add_q
        sum_kv[0] = add_k if start else sum_kv[0] + add_k
        sum_kv[1] = add_v if start else sum_kv[1] + add_v

    send_ax(1)
    send_ax(-1)
    send_ay(0, 1, 0)
    send_ay(0, -1, 0)
    pass_on(("ax", 2), part(ours, 0, 0), at_seg(2, 0))
    send_by(1, 0)
    send_by(-1, 0)
    send_bx(1, 0)
    send_wz(1, 0)
    send_wz(-1, 0)
    for dx in (3, 1, 2):
        wait_ax(dx)
        send_ay(dx, 1, 0)
        send_ay(dx, -1, 0)
        send_az(dx, 0)
    net.wait("up", mod.at[core, first], sibling)
    net.send("mod", "mod", mod.at[core, first], mod.at[core, first], sibling)
    net.wait("down", mod.at[core, last], sibling)
    net.send("mod", "mod", mod.at[core, last], mod.at[core, last], sibling)

    pair = lax.div(y, 2)
    side = 1 - 2 * lax.rem(y, 2)
    pairs = [pair, ring(pair - side, YN // 2), ring(pair + side, YN // 2), ring(pair + 2, YN // 2)]

    for far in range(1, top + 1):
        for way in (1, -1):
            if goes(way, far, True):
                wait_by(way, far)
                send_by(way, far)
                send_bx(way, far)
        for way in (1, -1):
            if relayed(far - 1) and (far > 1 or way == 1):
                relay_bx(way, far - 1)
        for dx in (0, 3, 1, 2):
            for way in (1, -1):
                if goes(way, far, False, dx):
                    wait_ay(dx, way, far)
                    send_ay(dx, way, far)
                    send_az(dx, -way * far)
        for way in (1, -1):
            if far < top or way == 1:
                take_wz(way, far)
        if far == 1:
            settle(0)
        elif far < top:
            if far == 2:
                net.wait("mod", mod.at[other], sibling)
                net.wait("size", sizes.at[other], sibling)
            settle(far - 1)
            project(pairs[far - 2], far == 2)

    for way, zs in ((1, slice(0, ZN // 2)), (-1, slice(ZN // 2, ZN))):
        net.send("wx", "wx", wt.at[near, zs, core], wt.at[near, zs, core], at_seg(way, 0))
    net.send("ws", "ws", wt.at[near, :, core], wt.at[near, :, core], sibling)
    settle(top - 1)
    project(pairs[2], False)
    settle(top)
    project(pairs[3], False)
    for c in range(3):
        cols = slice(c * 128, (c + 1) * 128)
        q[c] = (sum_q[:, cols].astype(BF16) * 0.125).astype(BF16).reshape(2, ROWS, 128)
        k[c] = sum_kv[0, :, cols].astype(BF16).reshape(2, KEYS, 128)
        v[c] = sum_kv[1, :, cols].astype(BF16).reshape(2, KEYS, 128)

    at_q = lax.broadcasted_iota(jnp.int32, (ROWS, KEYS), 0)
    at_k = lax.broadcasted_iota(jnp.int32, (ROWS, KEYS), 1)
    frame = seg * ROWS - HALO + at_k
    allowed = (at_k >= at_q) & (at_k <= at_q + 2 * HALO) & (frame >= 0) & (frame < SEGS * ROWS)
    bias = jnp.where(allowed, 0.0, -1e30).astype(F32)
    bias = jnp.concatenate([bias, bias], axis=0)
    lane = lax.broadcasted_iota(jnp.int32, (ROWS, 128), 1)
    ones = jnp.ones((KEYS, 128), BF16)
    for c in range(3):
        total = None
        for s in range(2):
            asked = q[c, s]
            nothing = jnp.zeros_like(asked)
            both = jnp.concatenate([jnp.where(lane < 64, asked, nothing), jnp.where(lane < 64, nothing, asked)], axis=0)
            scores = dot(both, k[c, s], ((1,), (1,))) + bias
            lifted = jnp.exp(scores - jnp.max(scores, axis=1, keepdims=True)).astype(BF16)
            got = dot(lifted, v[c, s]) / dot(lifted, ones)
            got = jnp.where(lane < 64, got[:ROWS], got[ROWS:]).astype(BF16)
            term = got.astype(F32) * sizes[s, 0:1, :]
            if s == 0:
                own_t[:, c * 128 : (c + 1) * 128] = term.astype(BF16)
                total = term
            else:
                total = total + term
        give[:, c * 128 : (c + 1) * 128] = total.astype(BF16)

    share = ROWS // ZN

    def share_rows(i):
        return pl.ds(pl.multiple_of(i * share, share), share)

    for dz in (4, 3, 5, 2, 6, 1, 7):
        net.send("there", "there", give.at[share_rows(ring(z + dz, ZN))], parts.at[z], at_z(dz))
    parts[z] = give[share_rows(z), :]
    net.wait("wx", wt.at[1 - near, :, core], sibling)
    net.send("ws", "ws", wt.at[1 - near, :, core], wt.at[1 - near, :, core], sibling)
    net.wait("there", parts.at[0 : ZN - 1], sibling)
    total = jnp.zeros((share, HALF), F32)
    for i in range(ZN):
        sums[i] = total.astype(BF16)
        total = total + parts[i].astype(F32)
    for dz in (4, 3, 5, 2, 6, 1, 7):
        net.send("back", "back", sums.at[ring(z + dz, ZN)], before.at[share_rows(z)], at_z(dz))
    before[share_rows(z), :] = sums[z]
    net.wait("ws", wt.at[:, :, other], sibling)
    net.wait("back", before.at[0 : ROWS - share], sibling)

    even = before[...]
    odd = (even.astype(F32) + own_t[...].astype(F32)).astype(BF16)
    full[core] = jnp.where(core == 0, even, odd)
    own_t[...] = jnp.where(core == 0, odd, even)
    net.send("full", "full", own_t, full.at[core], sibling)
    drift = dot(full[core], wt[core].reshape(D, HALF), ((1,), (1,)))
    net.wait("full", full.at[other], sibling)
    drift = drift + dot(full[other], wt[other].reshape(D, HALF), ((1,), (1,)))
    out[...] = (noise[...].astype(F32) + drift).astype(BF16)

    net.sent("z", slots.at[0 : STEPS - 1], sibling)
    net.sent("mod", mod.at[:, 0 : HALO + ROWS], sibling)
    net.sent("size", sizes.at[0], sibling)
    net.sent("w", blocks(net.count["w"]), sibling)
    net.sent("wz", wt.at[0, 0 : ZN - 1, 0], sibling)
    net.sent("wx", wt.at[0, :, 0], sibling)
    net.sent("ws", wt.at[:, :, 0], sibling)
    net.sent("there", parts.at[0 : ZN - 1], sibling)
    net.sent("back", parts.at[0 : ZN - 1], sibling)
    net.sent("full", own_t, sibling)


def shards(trajectory, noise, mod_shift, mod_scale, step_size, prompt_table, prompt_map, w_qkv, w_out):
    vmem = pl.BlockSpec(memory_space=pltpu.VMEM)
    smem = pl.BlockSpec(memory_space=pltpu.SMEM)
    hbm = pl.BlockSpec(memory_space=pl.ANY)
    result = pl.pallas_call(
        kernel,
        out_shape=jax.ShapeDtypeStruct((ROWS, D), BF16),
        in_specs=[hbm, hbm, hbm, hbm, smem, hbm, hbm, hbm, hbm],
        out_specs=vmem,
        scratch_shapes=[
            pltpu.VMEM((1, ROWS, D), BF16),
            pltpu.VMEM((ROWS, D), BF16),
            pltpu.VMEM((1, D), F32),
            pltpu.VMEM((1, D), F32),
            pltpu.VMEM((8, D), F32),
            pltpu.VMEM((1, ROWS), jnp.int32),
            pltpu.VMEM((SHARD, 3 * HQ), BF16),
            pltpu.VMEM((2, SLOT, 128), F32),
            pltpu.VMEM((2, SLOT, 128), BF16),
            pltpu.VMEM((STEPS, SLOT, 128), BF16),
            pltpu.VMEM((CHUNKS * BLOCK, STEPS * SLOT), BF16),
            pltpu.VMEM((3, D, HALF), BF16),
            pltpu.VMEM((2, ZN, 2, WO, HALF), BF16),
            pltpu.VMEM((2, KEYS, D), BF16),
            pltpu.VMEM((2, 8, 128), F32),
            pltpu.VMEM((2 * ROWS, HALF), F32),
            pltpu.VMEM((2, 2 * KEYS, HALF), F32),
            pltpu.VMEM((3, 2, ROWS, 128), BF16),
            pltpu.VMEM((3, 2, KEYS, 128), BF16),
            pltpu.VMEM((3, 2, KEYS, 128), BF16),
            pltpu.VMEM((ROWS, HALF), BF16),
            pltpu.VMEM((ZN, ROWS // ZN, HALF), BF16),
            pltpu.VMEM((ZN, ROWS // ZN, HALF), BF16),
            pltpu.VMEM((ROWS, HALF), BF16),
            pltpu.VMEM((ROWS, HALF), BF16),
            pltpu.VMEM((2, ROWS, HALF), BF16),
            pltpu.SemaphoreType.DMA((8,)),
            pltpu.SemaphoreType.DMA((SENDS,)),
            pltpu.SemaphoreType.DMA((RECVS,)),
        ],
        compiler_params=pltpu.CompilerParams(
            collective_id=0, has_side_effects=True, vmem_limit_bytes=60 * 1024 * 1024
        ),
    )(
        trajectory, noise, mod_shift, mod_scale, step_size, prompt_table,
        prompt_map.reshape(1, ROWS), w_qkv, w_out.T,
    )
    return result[None]


def solution(mesh):
    return jax.shard_map(
        shards,
        mesh=mesh,
        in_specs=(
            P("step", "seg", None),
            P("seg", None),
            P("step", None),
            P("step", None),
            P("step"),
            P(),
            P("seg"),
            P(("seg", "step"), None),
            P(None, "step"),
        ),
        out_specs=P("step", "seg", None),
        check_vma=False,
    )
```

```python
import functools

import jax
import jax.numpy as jnp
from jax import lax
from jax.experimental import pallas as pl
from jax.experimental.pallas import tpu as pltpu
from jax.sharding import PartitionSpec as P

MESH = pl.DeviceIdType.MESH
BF16 = jnp.bfloat16
F32 = jnp.float32
XN, YN, ZN = 4, 8, 8
SEGS, STEPS = XN * YN, 2 * ZN
ROWS, HALO, D, HQ = 128, 64, 1536, 768
KEYS = ROWS + 2 * HALO
HALF = HQ // 2
CHUNKS = 9
SHARD = 3
BLOCK = SHARD * STEPS
SLOT = 32
WO = D // STEPS
PAIR = 2 * XN * BLOCK
SENDS, RECVS = 12, 80


def dot(a, b, contract=((1,), (0,)), precision=None):
    return lax.dot_general(a, b, (contract, ((), ())), preferred_element_type=F32, precision=precision)


class Net:
    def __init__(self, send, recv):
        self.sems, self.index, self.count = (send, recv), ({}, {}), {}

    def sem(self, side, name):
        index = self.index[side]
        return self.sems[side].at[index.setdefault(name, len(index))]

    def send(self, group, name, src, dst, device):
        self.count[group] = self.count.get(group, 0) + 1
        pltpu.make_async_remote_copy(
            src_ref=src, dst_ref=dst, send_sem=self.sem(0, group), recv_sem=self.sem(1, name),
            device_id=device, device_id_type=MESH,
        ).start()

    def wait(self, name, ref, device):
        pltpu.make_async_remote_copy(
            src_ref=ref, dst_ref=ref, send_sem=self.sems[0].at[0], recv_sem=self.sem(1, name),
            device_id=device, device_id_type=MESH,
        ).wait_recv()

    def sent(self, group, ref, device):
        pltpu.make_async_remote_copy(
            src_ref=ref, dst_ref=ref, send_sem=self.sem(0, group), recv_sem=self.sems[1].at[0],
            device_id=device, device_id_type=MESH,
        ).wait_send()


def kernel(
    traj_hbm, noise_hbm, shift_hbm, scale_hbm, size, table_hbm, pmap_hbm, wq_hbm, wo_hbm, out,
    traj, noise, shift, scale, table, pmap, wq, stage, shard, slots, perm, w, wt, mod, sizes,
    sum_q, sum_kv, q, k, v, own_t, parts, sums, before, give, full, extra, start, load, send, recv,
):
    seg, step = lax.axis_index("seg"), lax.axis_index("step")
    x, y, core, z = lax.rem(seg, XN), lax.div(seg, XN), lax.rem(step, 2), lax.div(step, 2)
    other = 1 - core
    net = Net(send, recv)

    def ring(i, n):
        return lax.rem(i + n, n)

    def seg_of(dx, dy):
        return ring(y + dy, YN) * XN + ring(x + dx, XN)

    def at_seg(dx, dy):
        return (seg_of(dx, dy), step)

    def at_z(dz):
        return (seg, ring(z + dz, ZN) * 2 + core)

    sibling = (seg, z * 2 + other)
    following, preceding = (ring(seg + 1, SEGS), step), (ring(seg - 1, SEGS), step)

    peers = [(seg, ring(step + i, STEPS)) for i in range(1, STEPS)]
    peers += [at_seg(i, j) for i in range(XN) for j in (0, 1, -1) if (i, j) != (0, 0)]
    peers += [at_seg(0, 2), at_seg(0, -2), following, preceding]
    barrier = pltpu.get_barrier_semaphore()
    for peer in peers:
        pl.semaphore_signal(barrier, inc=1, device_id=peer, device_id_type=MESH)

    near = lax.rem(x, 2)

    def wt_block(dz):
        return wt.at[near, ring(z + dz, ZN), core]

    sources = [
        (wq_hbm, wq), (traj_hbm, traj), (pmap_hbm, pmap), (table_hbm, table), (shift_hbm, shift), (scale_hbm, scale),
        (wo_hbm.at[:, pl.ds(pl.multiple_of(near * HALF, HALF), HALF)], wt_block(0)), (noise_hbm, noise),
    ]
    loads = [pltpu.make_async_copy(src, dst, load.at[i]) for i, (src, dst) in enumerate(sources)]
    for copy in loads:
        copy.start()

    stage[...] = jnp.zeros_like(stage)
    loads[0].wait()
    rows = wq[...].astype(F32)
    for half in range(2):
        for c in range(CHUNKS):
            col = ((c // 3) * 6 + half * 3 + c % 3) * 128
            stage[half, c * SHARD : (c + 1) * SHARD, :] = rows[:, col : col + 128]
    shard[...] = stage[...].astype(BF16)
    slots[step] = shard[core]
    pl.semaphore_wait(barrier, len(peers))

    for dz in (4, 3, 5, 2, 6, 1, 7, 0):
        for swap in range(2):
            if (dz, swap) == (0, 0):
                continue
            there = lax.rem(core + swap, 2)
            net.send("z", "z", shard.at[there], slots.at[step], (seg, ring(z + dz, ZN) * 2 + there))

    mine, low, high = (slice(HALO, HALO + ROWS), slice(HALO, 2 * HALO), slice(ROWS, ROWS + HALO))
    first, last = slice(0, HALO), slice(HALO + ROWS, KEYS)
    for copy in loads[1:]:
        copy.wait()
    whole = table[...]
    upper = whole.astype(BF16)
    rest = whole - upper.astype(F32)
    middle = rest.astype(BF16)
    lower = (rest - middle.astype(F32)).astype(BF16)
    onehot = (lax.broadcasted_iota(jnp.int32, (8, ROWS), 0) == pmap[...]).astype(F32)
    onehot = jnp.concatenate([onehot, onehot, onehot], axis=0).astype(BF16)
    chosen = dot(onehot, jnp.concatenate([upper, middle, lower], axis=0), ((0,), (0,)))
    inputs = traj[0].astype(F32) + chosen
    center = jnp.mean(inputs, axis=-1, keepdims=True)
    inputs = inputs - center
    spread = jnp.mean(jnp.square(inputs), axis=-1, keepdims=True)
    normed = inputs * lax.rsqrt(spread + 1e-06)
    mod[core, mine, :] = (normed * (1.0 + scale[...]) + shift[...]).astype(BF16)
    sizes[core] = jnp.full((8, 128), size[0], F32)
    net.send("mod", "up", mod.at[core, high], mod.at[core, first], following)
    net.send("mod", "down", mod.at[core, low], mod.at[core, last], preceding)
    net.send("mod", "mod", mod.at[core, mine], mod.at[core, mine], sibling)
    net.send("size", "size", sizes.at[core], sizes.at[core], sibling)

    shape = (BLOCK, STEPS * SLOT)
    i = lax.broadcasted_iota(jnp.int32, shape, 0)
    third = lax.shift_right_logical(i * 43, 7)
    j = lax.broadcasted_iota(jnp.int32, shape, 1) - third * SLOT - (i - third * SHARD)
    for c in range(CHUNKS):
        perm[c * BLOCK : (c + 1) * BLOCK, :] = jnp.where(j == c * SHARD, 1.0, 0.0).astype(BF16)
    net.wait("z", slots.at[0 : STEPS - 1], sibling)
    block = dot(perm[...], slots[...].reshape(STEPS * SLOT, 128)).astype(BF16)

    ours = 1 + lax.rem(z, 2)

    def part(which, dx, dy):
        return w.at[which, pl.ds(pl.multiple_of(seg_of(dx, dy) * BLOCK, BLOCK), BLOCK)]

    def blocks(n):
        return w.at[:, 0 : n * BLOCK // 3]

    for c in range(CHUNKS):
        own_rows = pl.ds(pl.multiple_of(seg * BLOCK, BLOCK), BLOCK)
        w[c // 3, own_rows, (c % 3) * 128 : (c % 3 + 1) * 128] = block[c * BLOCK : (c + 1) * BLOCK]

    def pass_on(name, ref, device):
        net.send("w", name, ref, ref, device)

    top = YN // 2

    def goes(way, far, is_b, dx=0):
        return far < top or (way == 1) == (is_b or dx % 2 == 0)

    def send_a(dx, way):
        name = ("ay", -dx % XN, way, 1) if way else ("ax", -dx % XN)
        pass_on(name, part(ours, 0, 0), at_seg(dx, way))

    def wait_ax(dx):
        net.wait(("ax", dx % XN), part(ours, dx, 0), sibling)

    def send_ay(dx, way, far):
        ref = part(ours, dx, -way * far)
        if far + 1 < top:
            pass_on(("ay", dx, way, far + 1), ref, at_seg(0, way))
        if far + 2 == top and goes(way, top, False, dx):
            pass_on(("ay", dx, way, top), ref, at_seg(0, 2 * way))

    def wait_ay(dx, way, far):
        net.wait(("ay", dx, way, far), part(ours, dx, -way * far), sibling)

    def send_az(dx, dy):
        pass_on(("az", abs(dy)), part(ours, dx, dy), at_z(1 if dx % 2 == 0 else -1))

    def send_by(way, far, hops):
        if far + hops < top or goes(way, top, True):
            pass_on(("by", way, far + hops), part(0, 0, -way * far), at_seg(0, hops * way))

    def wait_by(way, far):
        net.wait(("by", way, far), part(0, 0, -way * far), sibling)

    def relayed(far):
        return far < top - 1

    def send_bx(way_y, far):
        dy = -way_y * far
        relay = way_y if relayed(far) else 0
        for way in (1, -1):
            pass_on(("bxr", dy) if way == relay else ("bx", far), part(0, 0, dy), at_seg(way, 0))
        if not relay:
            pass_on(("bx", far), part(0, 0, dy), at_seg(2, 0))

    def relay_bx(way_y, far):
        dy = -way_y * far
        net.wait(("bxr", dy), part(0, -way_y, dy), sibling)
        pass_on(("bx", far), part(0, -way_y, dy), at_seg(way_y, 0))

    def settle(far):
        both = 2 if 0 < far < top else 1
        net.wait(("bx", far), blocks(both * (2 if relayed(far) else 3)), sibling)
        net.wait(("az", far), blocks(both * XN - (far == 0)), sibling)

    def send_wz(way, far):
        if far + 1 < ZN // 2 or (far + 1 == ZN // 2 and way == 1):
            net.send("wz", ("wz", way, far + 1), wt_block(-way * far), wt_block(-way * far), at_z(way))

    def take_wz(way, far):
        net.wait(("wz", way, far), wt_block(-way * far), sibling)
        send_wz(way, far)

    def project(pair, start):
        rows = pl.ds(pl.multiple_of(pair * PAIR, PAIR), PAIR)
        everyone = mod[:, :, rows].reshape(2 * KEYS, PAIR)
        asked = mod[:, mine, rows].reshape(2 * ROWS, PAIR)
        add_q, add_k, add_v = dot(asked, w[0, rows]), dot(everyone, w[1, rows]), dot(everyone, w[2, rows])
        sum_q[...] = add_q if start else sum_q[...] + add_q
        sum_kv[0] = add_k if start else sum_kv[0] + add_k
        sum_kv[1] = add_v if start else sum_kv[1] + add_v

    for dx in (0, 1, 3, 2):
        send_a(dx, 1)
        send_a(dx, -1)
    for hops in (1, 2):
        send_by(1, 0, hops)
        send_by(-1, 0, hops)
    for dx in (1, 3, 2):
        send_a(dx, 0)
    send_bx(1, 0)
    send_wz(1, 0)
    send_wz(-1, 0)

    pair = lax.div(y, 2)
    side = 1 - 2 * lax.rem(y, 2)
    pairs = [pair, ring(pair - side, YN // 2), ring(pair + side, YN // 2), ring(pair + 2, YN // 2)]

    def take_ay(fars):
        for far in fars:
            for dx in (0, 3, 1, 2):
                for way in (1, -1):
                    if goes(way, far, False, dx):
                        wait_ay(dx, way, far)
                        send_ay(dx, way, far)
                        send_az(dx, -way * far)

    def take_by(fars):
        for far in fars:
            for way in (1, -1):
                if goes(way, far, True):
                    wait_by(way, far)
                    if far == 2:
                        send_by(way, far, 1)
                        send_by(way, far, 2)
                    send_bx(way, far)

    take_ay((1,))
    take_by((1, 2))
    for dx in (3, 1, 2):
        wait_ax(dx)
        send_az(dx, 0)
    relay_bx(1, 0)
    net.wait("up", mod.at[core, first], sibling)
    net.send("mod", "mod", mod.at[core, first], mod.at[core, first], sibling)
    net.wait("down", mod.at[core, last], sibling)
    net.send("mod", "mod", mod.at[core, last], mod.at[core, last], sibling)
    take_wz(1, 1)
    take_wz(-1, 1)

    take_ay((2,))
    relay_bx(1, 1)
    relay_bx(-1, 1)
    take_by((3, 4))
    relay_bx(1, 2)
    relay_bx(-1, 2)
    settle(0)
    net.wait("mod", mod.at[other], sibling)
    net.wait("size", sizes.at[other], sibling)
    take_wz(1, 2)
    take_wz(-1, 2)

    take_ay((3, 4))
    settle(1)
    project(pairs[0], True)
    take_wz(1, 3)
    take_wz(-1, 3)
    settle(2)
    project(pairs[1], False)
    take_wz(1, 4)

    for way, zs in ((1, slice(0, ZN // 2)), (-1, slice(ZN // 2, ZN))):
        net.send("wx", "wx", wt.at[near, zs, core], wt.at[near, zs, core], at_seg(way, 0))
    net.send("ws", "ws", wt.at[near, :, core], wt.at[near, :, core], sibling)
    settle(top - 1)
    project(pairs[2], False)
    settle(top)
    project(pairs[3], False)
    for c in range(3):
        cols = slice(c * 128, (c + 1) * 128)
        q[c] = (sum_q[:, cols].astype(BF16) * 0.125).astype(BF16).reshape(2, ROWS, 128)
        k[c] = sum_kv[0, :, cols].astype(BF16).reshape(2, KEYS, 128)
        v[c] = sum_kv[1, :, cols].astype(BF16).reshape(2, KEYS, 128)

    at_q = lax.broadcasted_iota(jnp.int32, (ROWS, KEYS), 0)
    at_k = lax.broadcasted_iota(jnp.int32, (ROWS, KEYS), 1)
    frame = seg * ROWS - HALO + at_k
    allowed = (at_k >= at_q) & (at_k <= at_q + 2 * HALO) & (frame >= 0) & (frame < SEGS * ROWS)
    bias = jnp.where(allowed, 0.0, -1e30).astype(F32)
    bias = jnp.concatenate([bias, bias], axis=0)
    lane = lax.broadcasted_iota(jnp.int32, (ROWS, 128), 1)
    ones = jnp.ones((KEYS, 128), BF16)
    for c in range(3):
        total = None
        for s in range(2):
            asked = q[c, s]
            nothing = jnp.zeros_like(asked)
            both = jnp.concatenate([jnp.where(lane < 64, asked, nothing), jnp.where(lane < 64, nothing, asked)], axis=0)
            scores = dot(both, k[c, s], ((1,), (1,))) + bias
            lifted = jnp.exp(scores - jnp.max(scores, axis=1, keepdims=True)).astype(BF16)
            got = dot(lifted, v[c, s]) / dot(lifted, ones)
            got = jnp.where(lane < 64, got[:ROWS], got[ROWS:]).astype(BF16)
            term = got.astype(F32) * sizes[s, 0:1, :]
            if s == 0:
                own_t[:, c * 128 : (c + 1) * 128] = term.astype(BF16)
                total = term
            else:
                total = total + term
        give[:, c * 128 : (c + 1) * 128] = total.astype(BF16)

    share = ROWS // ZN

    def share_rows(i):
        return pl.ds(pl.multiple_of(i * share, share), share)

    net.send("own", "own", own_t, extra.at[core], sibling)
    for dz in (4, 3, 5, 2, 6, 1, 7):
        net.send("there", "there", give.at[share_rows(ring(z + dz, ZN))], parts.at[z], at_z(dz))
    parts[z] = give[share_rows(z), :]
    net.wait("wx", wt.at[1 - near, :, core], sibling)
    net.send("ws", "ws", wt.at[1 - near, :, core], wt.at[1 - near, :, core], sibling)
    net.wait("there", parts.at[0 : ZN - 1], sibling)
    total = jnp.zeros((share, HALF), F32)
    for i in range(ZN):
        sums[i] = total.astype(BF16)
        total = total + parts[i].astype(F32)
    for dz in (4, 3, 5, 2, 6, 1, 7):
        net.send("back", "back", sums.at[ring(z + dz, ZN)], before.at[share_rows(z)], at_z(dz))
    before[share_rows(z), :] = sums[z]
    net.wait("ws", wt.at[:, :, other], sibling)
    net.wait("own", extra.at[other], sibling)
    odd = jnp.where(core == 0, jnp.zeros((ROWS, HALF), BF16), extra[other])
    base = dot(odd, wt[other].reshape(D, HALF), ((1,), (1,)))
    odd = jnp.where(core == 0, jnp.zeros((ROWS, HALF), BF16), own_t[...])
    start[...] = noise[...].astype(F32) + base + dot(odd, wt[core].reshape(D, HALF), ((1,), (1,)))
    net.wait("back", before.at[0 : ROWS - share], sibling)

    net.send("full", "full", before, full.at[core], sibling)
    start[...] += dot(before[...], wt[core].reshape(D, HALF), ((1,), (1,)))
    net.wait("full", full.at[other], sibling)
    out[...] = (start[...] + dot(full[other], wt[other].reshape(D, HALF), ((1,), (1,)))).astype(BF16)

    net.sent("z", slots.at[0 : STEPS - 1], sibling)
    net.sent("mod", mod.at[:, 0 : HALO + ROWS], sibling)
    net.sent("size", sizes.at[0], sibling)
    net.sent("w", blocks(net.count["w"]), sibling)
    net.sent("wz", wt.at[0, 0 : ZN - 1, 0], sibling)
    net.sent("wx", wt.at[0, :, 0], sibling)
    net.sent("ws", wt.at[:, :, 0], sibling)
    net.sent("there", parts.at[0 : ZN - 1], sibling)
    net.sent("back", parts.at[0 : ZN - 1], sibling)
    net.sent("own", own_t, sibling)
    net.sent("full", before, sibling)


def shards(trajectory, noise, mod_shift, mod_scale, step_size, prompt_table, prompt_map, w_qkv, w_out):
    vmem = pl.BlockSpec(memory_space=pltpu.VMEM)
    smem = pl.BlockSpec(memory_space=pltpu.SMEM)
    hbm = pl.BlockSpec(memory_space=pl.ANY)
    result = pl.pallas_call(
        kernel,
        out_shape=jax.ShapeDtypeStruct((ROWS, D), BF16),
        in_specs=[hbm, hbm, hbm, hbm, smem, hbm, hbm, hbm, hbm],
        out_specs=vmem,
        scratch_shapes=[
            pltpu.VMEM((1, ROWS, D), BF16),
            pltpu.VMEM((ROWS, D), BF16),
            pltpu.VMEM((1, D), F32),
            pltpu.VMEM((1, D), F32),
            pltpu.VMEM((8, D), F32),
            pltpu.VMEM((1, ROWS), jnp.int32),
            pltpu.VMEM((SHARD, 3 * HQ), BF16),
            pltpu.VMEM((2, SLOT, 128), F32),
            pltpu.VMEM((2, SLOT, 128), BF16),
            pltpu.VMEM((STEPS, SLOT, 128), BF16),
            pltpu.VMEM((CHUNKS * BLOCK, STEPS * SLOT), BF16),
            pltpu.VMEM((3, D, HALF), BF16),
            pltpu.VMEM((2, ZN, 2, WO, HALF), BF16),
            pltpu.VMEM((2, KEYS, D), BF16),
            pltpu.VMEM((2, 8, 128), F32),
            pltpu.VMEM((2 * ROWS, HALF), F32),
            pltpu.VMEM((2, 2 * KEYS, HALF), F32),
            pltpu.VMEM((3, 2, ROWS, 128), BF16),
            pltpu.VMEM((3, 2, KEYS, 128), BF16),
            pltpu.VMEM((3, 2, KEYS, 128), BF16),
            pltpu.VMEM((ROWS, HALF), BF16),
            pltpu.VMEM((ZN, ROWS // ZN, HALF), BF16),
            pltpu.VMEM((ZN, ROWS // ZN, HALF), BF16),
            pltpu.VMEM((ROWS, HALF), BF16),
            pltpu.VMEM((ROWS, HALF), BF16),
            pltpu.VMEM((2, ROWS, HALF), BF16),
            pltpu.VMEM((2, ROWS, HALF), BF16),
            pltpu.VMEM((ROWS, D), F32),
            pltpu.SemaphoreType.DMA((8,)),
            pltpu.SemaphoreType.DMA((SENDS,)),
            pltpu.SemaphoreType.DMA((RECVS,)),
        ],
        compiler_params=pltpu.CompilerParams(
            collective_id=0, has_side_effects=True, vmem_limit_bytes=60 * 1024 * 1024
        ),
    )(
        trajectory, noise, mod_shift, mod_scale, step_size, prompt_table,
        prompt_map.reshape(1, ROWS), w_qkv, w_out.T,
    )
    return result[None]


def solution(mesh):
    return jax.shard_map(
        shards,
        mesh=mesh,
        in_specs=(
            P("step", "seg", None),
            P("seg", None),
            P("step", None),
            P("step", None),
            P("step"),
            P(),
            P("seg"),
            P(("seg", "step"), None),
            P(None, "step"),
        ),
        out_specs=P("step", "seg", None),
        check_vma=False,
    )
```

```python
import functools

import jax
import jax.numpy as jnp
from jax import lax
from jax.experimental import pallas as pl
from jax.experimental.pallas import tpu as pltpu
from jax.sharding import PartitionSpec as P

MESH = pl.DeviceIdType.MESH
BF16 = jnp.bfloat16
F32 = jnp.float32
XN, YN, ZN = 4, 8, 8
SEGS, STEPS = XN * YN, 2 * ZN
ROWS, HALO, D, HQ = 128, 64, 1536, 768
KEYS = ROWS + 2 * HALO
HALF = HQ // 2
CHUNKS = 9
SHARD = 3
BLOCK = SHARD * STEPS
SLOT = 32
WO = D // STEPS
PAIR = 2 * XN * BLOCK
SENDS, RECVS = 11, 85


def dot(a, b, contract=((1,), (0,)), precision=None):
    return lax.dot_general(a, b, (contract, ((), ())), preferred_element_type=F32, precision=precision)


class Net:
    def __init__(self, send, recv):
        self.sems, self.index, self.count = (send, recv), ({}, {}), {}

    def sem(self, side, name):
        index = self.index[side]
        return self.sems[side].at[index.setdefault(name, len(index))]

    def send(self, group, name, src, dst, device):
        self.count[group] = self.count.get(group, 0) + 1
        pltpu.make_async_remote_copy(
            src_ref=src, dst_ref=dst, send_sem=self.sem(0, group), recv_sem=self.sem(1, name),
            device_id=device, device_id_type=MESH,
        ).start()

    def wait(self, name, ref, device):
        pltpu.make_async_remote_copy(
            src_ref=ref, dst_ref=ref, send_sem=self.sems[0].at[0], recv_sem=self.sem(1, name),
            device_id=device, device_id_type=MESH,
        ).wait_recv()

    def sent(self, group, ref, device):
        pltpu.make_async_remote_copy(
            src_ref=ref, dst_ref=ref, send_sem=self.sem(0, group), recv_sem=self.sems[1].at[0],
            device_id=device, device_id_type=MESH,
        ).wait_send()


def kernel(
    traj_hbm, noise_hbm, shift_hbm, scale_hbm, size, table_hbm, pmap_hbm, wq_hbm, wo_hbm, out,
    traj, noise, shift, scale, table, pmap, wq, stage, shard, slots, perm, w, wt, mod, sizes,
    sum_q, sum_kv, q, k, v, own_t, parts, sums, before, give, full, extra, start, load, send, recv,
):
    seg, step = lax.axis_index("seg"), lax.axis_index("step")
    x, y, core, z = lax.rem(seg, XN), lax.div(seg, XN), lax.rem(step, 2), lax.div(step, 2)
    other = 1 - core
    net = Net(send, recv)

    def ring(i, n):
        return lax.rem(i + n, n)

    def seg_of(dx, dy):
        return ring(y + dy, YN) * XN + ring(x + dx, XN)

    def at_seg(dx, dy):
        return (seg_of(dx, dy), step)

    def at_z(dz):
        return (seg, ring(z + dz, ZN) * 2 + core)

    sibling = (seg, z * 2 + other)
    following, preceding = (ring(seg + 1, SEGS), step), (ring(seg - 1, SEGS), step)

    peers = [(seg, ring(step + i, STEPS)) for i in range(1, STEPS)]
    peers += [at_seg(i, 0) for i in range(1, XN)] + [at_seg(0, i) for i in (1, -1, 2, -2)] + [following, preceding]
    barrier = pltpu.get_barrier_semaphore()
    for peer in peers:
        pl.semaphore_signal(barrier, inc=1, device_id=peer, device_id_type=MESH)

    near = lax.rem(x, 2)

    def wt_block(dz):
        return wt.at[near, ring(z + dz, ZN), core]

    sources = [
        (wq_hbm, wq), (traj_hbm, traj), (pmap_hbm, pmap), (table_hbm, table), (shift_hbm, shift), (scale_hbm, scale),
        (wo_hbm.at[:, pl.ds(pl.multiple_of(near * HALF, HALF), HALF)], wt_block(0)), (noise_hbm, noise),
    ]
    loads = [pltpu.make_async_copy(src, dst, load.at[i]) for i, (src, dst) in enumerate(sources)]
    for copy in loads:
        copy.start()

    stage[...] = jnp.zeros_like(stage)
    loads[0].wait()
    rows = wq[...].astype(F32)
    for half in range(2):
        for c in range(CHUNKS):
            col = ((c // 3) * 6 + half * 3 + c % 3) * 128
            stage[half, c * SHARD : (c + 1) * SHARD, :] = rows[:, col : col + 128]
    shard[...] = stage[...].astype(BF16)
    slots[step] = shard[core]
    pl.semaphore_wait(barrier, len(peers))

    for dz in (4, 3, 5, 2, 6, 1, 7, 0):
        for swap in range(2):
            if (dz, swap) == (0, 0):
                continue
            there = lax.rem(core + swap, 2)
            net.send("z", "z", shard.at[there], slots.at[step], (seg, ring(z + dz, ZN) * 2 + there))

    def send_wz(way, far):
        if far + 1 < ZN // 2 or (far + 1 == ZN // 2 and way == 1):
            net.send("wz", ("wz", way, far + 1), wt_block(-way * far), wt_block(-way * far), at_z(way))

    def take_wz(way, far):
        net.wait(("wz", way, far), wt_block(-way * far), sibling)
        send_wz(way, far)

    mine, low, high = (slice(HALO, HALO + ROWS), slice(HALO, 2 * HALO), slice(ROWS, ROWS + HALO))
    first, last = slice(0, HALO), slice(HALO + ROWS, KEYS)
    for copy in loads[1:]:
        copy.wait()
    send_wz(1, 0)
    send_wz(-1, 0)
    whole = table[...]
    upper = whole.astype(BF16)
    rest = whole - upper.astype(F32)
    middle = rest.astype(BF16)
    lower = (rest - middle.astype(F32)).astype(BF16)
    onehot = (lax.broadcasted_iota(jnp.int32, (8, ROWS), 0) == pmap[...]).astype(F32)
    onehot = jnp.concatenate([onehot, onehot, onehot], axis=0).astype(BF16)
    chosen = dot(onehot, jnp.concatenate([upper, middle, lower], axis=0), ((0,), (0,)))
    inputs = traj[0].astype(F32) + chosen
    center = jnp.mean(inputs, axis=-1, keepdims=True)
    inputs = inputs - center
    spread = jnp.mean(jnp.square(inputs), axis=-1, keepdims=True)
    normed = inputs * lax.rsqrt(spread + 1e-06)
    mod[core, mine, :] = (normed * (1.0 + scale[...]) + shift[...]).astype(BF16)
    sizes[core] = jnp.full((8, 128), size[0], F32)
    net.send("mod", "up", mod.at[core, high], mod.at[core, first], following)
    net.send("mod", "down", mod.at[core, low], mod.at[core, last], preceding)
    net.send("mod", "mod", mod.at[core, mine], mod.at[core, mine], sibling)
    net.send("size", "size", sizes.at[core], sizes.at[core], sibling)

    shape = (BLOCK, STEPS * SLOT)
    i = lax.broadcasted_iota(jnp.int32, shape, 0)
    third = lax.shift_right_logical(i * 43, 7)
    j = lax.broadcasted_iota(jnp.int32, shape, 1) - third * SLOT - (i - third * SHARD)
    for c in range(CHUNKS):
        perm[c * BLOCK : (c + 1) * BLOCK, :] = jnp.where(j == c * SHARD, 1.0, 0.0).astype(BF16)
    net.wait("z", slots.at[0 : STEPS - 1], sibling)
    block = dot(perm[...], slots[...].reshape(STEPS * SLOT, 128)).astype(BF16)

    ours = 1 + lax.rem(z, 2)

    def part(which, dx, dy):
        return w.at[which, pl.ds(pl.multiple_of(seg_of(dx, dy) * BLOCK, BLOCK), BLOCK)]

    def blocks(n):
        return w.at[:, 0 : n * BLOCK // 3]

    for c in range(CHUNKS):
        own_rows = pl.ds(pl.multiple_of(seg * BLOCK, BLOCK), BLOCK)
        w[c // 3, own_rows, (c % 3) * 128 : (c % 3 + 1) * 128] = block[c * BLOCK : (c + 1) * BLOCK]

    def pass_on(name, ref, device):
        net.send("w", name, ref, ref, device)

    top = YN // 2

    def goes(way, far, is_b, dx=0):
        return far < top or (way == 1) == (is_b or dx % 2 == 0)

    def send_ax(dx):
        pass_on(("ax", -dx % XN), part(0, 0, 0), at_seg(dx, 0))

    def take_ax(dx):
        net.wait(("ax", dx % XN), part(0, dx, 0), sibling)
        send_ay(dx, 1, 0)
        send_ay(dx, -1, 0)

    def send_ay(dx, way, far):
        ref = part(0, dx, -way * far)
        if far + 1 < top:
            pass_on(("ay", dx, way, far + 1), ref, at_seg(0, way))
        if far + 2 == top and goes(way, top, False, dx):
            pass_on(("ay", dx, way, top), ref, at_seg(0, 2 * way))

    def take_ay(dx, far):
        for way in (1, -1):
            if goes(way, far, False, dx):
                net.wait(("ay", dx, way, far), part(0, dx, -way * far), sibling)
                send_ay(dx, way, far)

    def send_az(dx, dy):
        pass_on(("az", abs(dy)), part(ours, dx, dy), at_z(1 if dx % 2 == 0 else -1))

    def send_by(way, far, hops):
        if far + hops < top or goes(way, top, True):
            pass_on(("by", way, far + hops), part(ours, 0, -way * far), at_seg(0, hops * way))

    def take_by(far):
        for way in (1, -1):
            if goes(way, far, True):
                net.wait(("by", way, far), part(ours, 0, -way * far), sibling)
                if far == 2:
                    send_by(way, far, 1)
                    send_by(way, far, 2)
                send_bx(way, far)
                send_az(0, -way * far)

    def relayed(far):
        return 0 < far < top - 1

    def send_bx(way, far):
        for dx in (1, -1) if relayed(far) else (2, 1, -1):
            pass_on(("bx", -way * far, -dx % XN), part(ours, 0, -way * far), at_seg(dx, 0))

    def take_bx(far, opposite):
        for way in (1, -1):
            if not goes(way, far, True) or (far == 0 and way == -1):
                continue
            for dx in (2,) if opposite else (-way, way):
                ref = part(ours, dx, -way * far)
                net.wait(("bx", -way * far, dx % XN), ref, sibling)
                if relayed(far) and dx == -way:
                    pass_on(("bx", -way * far, 2), ref, at_seg(way, 0))
                send_az(dx, -way * far)

    def settle(far):
        net.wait(("az", far), blocks((2 if 0 < far < top else 1) * XN - (far == 0)), sibling)

    def project(pair, start):
        rows = pl.ds(pl.multiple_of(pair * PAIR, PAIR), PAIR)
        everyone = mod[:, :, rows].reshape(2 * KEYS, PAIR)
        asked = mod[:, mine, rows].reshape(2 * ROWS, PAIR)
        add_q, add_k, add_v = dot(asked, w[0, rows]), dot(everyone, w[1, rows]), dot(everyone, w[2, rows])
        sum_q[...] = add_q if start else sum_q[...] + add_q
        sum_kv[0] = add_k if start else sum_kv[0] + add_k
        sum_kv[1] = add_v if start else sum_kv[1] + add_v

    for dx in (1, -1, 2):
        send_ax(dx)
    for hops in (1, 2):
        send_by(1, 0, hops)
        send_by(-1, 0, hops)
    send_ay(0, 1, 0)
    send_ay(0, -1, 0)
    send_bx(1, 0)
    take_wz(1, 1)
    take_wz(-1, 1)

    pair = lax.div(y, 2)
    side = 1 - 2 * lax.rem(y, 2)
    pairs = [pair, ring(pair - side, YN // 2), ring(pair + side, YN // 2), ring(pair + 2, YN // 2)]

    for dx in (3, 1, 2):
        take_ax(dx)
    take_by(1)
    take_by(2)
    take_ay(0, 1)
    take_bx(0, False)
    net.wait("up", mod.at[core, first], sibling)
    net.send("mod", "mod", mod.at[core, first], mod.at[core, first], sibling)
    net.wait("down", mod.at[core, last], sibling)
    net.send("mod", "mod", mod.at[core, last], mod.at[core, last], sibling)
    take_wz(1, 2)
    take_wz(-1, 2)
    for dx in (3, 1, 2):
        take_ay(dx, 1)
    take_bx(1, False)
    take_bx(2, False)
    take_bx(0, True)
    take_by(3)
    take_by(4)
    take_wz(1, 3)
    take_wz(-1, 3)
    for dx in (0, 3, 1, 2):
        take_ay(dx, 2)
    take_bx(1, True)
    take_bx(2, True)
    for far in (3, 4):
        take_bx(far, False)
        take_bx(far, True)
    take_wz(1, 4)
    net.wait("mod", mod.at[other], sibling)
    net.wait("size", sizes.at[other], sibling)
    settle(0)
    settle(1)
    project(pairs[0], True)
    settle(2)
    project(pairs[1], False)
    for far in (3, 4):
        for dx in (0, 3, 1, 2):
            take_ay(dx, far)

    for way, zs in ((1, slice(0, ZN // 2)), (-1, slice(ZN // 2, ZN))):
        net.send("wx", "wx", wt.at[near, zs, core], wt.at[near, zs, core], at_seg(way, 0))
    net.send("ws", "ws", wt.at[near, :, core], wt.at[near, :, core], sibling)
    settle(top - 1)
    project(pairs[2], False)
    settle(top)
    project(pairs[3], False)
    for c in range(3):
        cols = slice(c * 128, (c + 1) * 128)
        q[c] = (sum_q[:, cols].astype(BF16) * 0.125).astype(BF16).reshape(2, ROWS, 128)
        k[c] = sum_kv[0, :, cols].astype(BF16).reshape(2, KEYS, 128)
        v[c] = sum_kv[1, :, cols].astype(BF16).reshape(2, KEYS, 128)

    at_q = lax.broadcasted_iota(jnp.int32, (ROWS, KEYS), 0)
    at_k = lax.broadcasted_iota(jnp.int32, (ROWS, KEYS), 1)
    frame = seg * ROWS - HALO + at_k
    allowed = (at_k >= at_q) & (at_k <= at_q + 2 * HALO) & (frame >= 0) & (frame < SEGS * ROWS)
    bias = jnp.where(allowed, 0.0, -1e30).astype(F32)
    bias = jnp.concatenate([bias, bias], axis=0)
    lane = lax.broadcasted_iota(jnp.int32, (ROWS, 128), 1)
    ones = jnp.ones((KEYS, 128), BF16)
    for c in range(3):
        total = None
        for s in range(2):
            asked = q[c, s]
            nothing = jnp.zeros_like(asked)
            both = jnp.concatenate([jnp.where(lane < 64, asked, nothing), jnp.where(lane < 64, nothing, asked)], axis=0)
            scores = dot(both, k[c, s], ((1,), (1,))) + bias
            lifted = jnp.exp(scores - jnp.max(scores, axis=1, keepdims=True)).astype(BF16)
            got = dot(lifted, v[c, s]) / dot(lifted, ones)
            got = jnp.where(lane < 64, got[:ROWS], got[ROWS:]).astype(BF16)
            term = got.astype(F32) * sizes[s, 0:1, :]
            if s == 0:
                own_t[:, c * 128 : (c + 1) * 128] = term.astype(BF16)
                total = term
            else:
                total = total + term
        give[:, c * 128 : (c + 1) * 128] = total.astype(BF16)

    share = ROWS // ZN

    def share_rows(i):
        return pl.ds(pl.multiple_of(i * share, share), share)

    net.send("own", "own", own_t, extra.at[core], sibling)
    for dz in (4, 3, 5, 2, 6, 1, 7):
        net.send("there", "there", give.at[share_rows(ring(z + dz, ZN))], parts.at[z], at_z(dz))
    parts[z] = give[share_rows(z), :]
    net.wait("wx", wt.at[1 - near, :, core], sibling)
    net.send("ws", "ws", wt.at[1 - near, :, core], wt.at[1 - near, :, core], sibling)
    net.wait("there", parts.at[0 : ZN - 1], sibling)
    total = jnp.zeros((share, HALF), F32)
    for i in range(ZN):
        sums[i] = total.astype(BF16)
        total = total + parts[i].astype(F32)
    for dz in (4, 3, 5, 2, 6, 1, 7):
        net.send("back", "back", sums.at[ring(z + dz, ZN)], before.at[share_rows(z)], at_z(dz))
    before[share_rows(z), :] = sums[z]
    net.wait("ws", wt.at[:, :, other], sibling)
    net.wait("own", extra.at[other], sibling)
    odd = jnp.where(core == 0, jnp.zeros((ROWS, HALF), BF16), extra[other])
    base = dot(odd, wt[other].reshape(D, HALF), ((1,), (1,)))
    odd = jnp.where(core == 0, jnp.zeros((ROWS, HALF), BF16), own_t[...])
    start[...] = noise[...].astype(F32) + base + dot(odd, wt[core].reshape(D, HALF), ((1,), (1,)))
    net.wait("back", before.at[0 : ROWS - share], sibling)

    net.send("full", "full", before, full.at[core], sibling)
    start[...] += dot(before[...], wt[core].reshape(D, HALF), ((1,), (1,)))
    net.wait("full", full.at[other], sibling)
    out[...] = (start[...] + dot(full[other], wt[other].reshape(D, HALF), ((1,), (1,)))).astype(BF16)

    net.sent("z", slots.at[0 : STEPS - 1], sibling)
    net.sent("mod", mod.at[:, 0 : HALO + ROWS], sibling)
    net.sent("size", sizes.at[0], sibling)
    net.sent("w", blocks(net.count["w"]), sibling)
    net.sent("wz", wt.at[0, 0 : ZN - 1, 0], sibling)
    net.sent("wx", wt.at[0, :, 0], sibling)
    net.sent("ws", wt.at[:, :, 0], sibling)
    net.sent("there", parts.at[0 : ZN - 1], sibling)
    net.sent("back", parts.at[0 : ZN - 1], sibling)
    net.sent("own", own_t, sibling)
    net.sent("full", before, sibling)


def shards(trajectory, noise, mod_shift, mod_scale, step_size, prompt_table, prompt_map, w_qkv, w_out):
    vmem = pl.BlockSpec(memory_space=pltpu.VMEM)
    smem = pl.BlockSpec(memory_space=pltpu.SMEM)
    hbm = pl.BlockSpec(memory_space=pl.ANY)
    result = pl.pallas_call(
        kernel,
        out_shape=jax.ShapeDtypeStruct((ROWS, D), BF16),
        in_specs=[hbm, hbm, hbm, hbm, smem, hbm, hbm, hbm, hbm],
        out_specs=vmem,
        scratch_shapes=[
            pltpu.VMEM((1, ROWS, D), BF16),
            pltpu.VMEM((ROWS, D), BF16),
            pltpu.VMEM((1, D), F32),
            pltpu.VMEM((1, D), F32),
            pltpu.VMEM((8, D), F32),
            pltpu.VMEM((1, ROWS), jnp.int32),
            pltpu.VMEM((SHARD, 3 * HQ), BF16),
            pltpu.VMEM((2, SLOT, 128), F32),
            pltpu.VMEM((2, SLOT, 128), BF16),
            pltpu.VMEM((STEPS, SLOT, 128), BF16),
            pltpu.VMEM((CHUNKS * BLOCK, STEPS * SLOT), BF16),
            pltpu.VMEM((3, D, HALF), BF16),
            pltpu.VMEM((2, ZN, 2, WO, HALF), BF16),
            pltpu.VMEM((2, KEYS, D), BF16),
            pltpu.VMEM((2, 8, 128), F32),
            pltpu.VMEM((2 * ROWS, HALF), F32),
            pltpu.VMEM((2, 2 * KEYS, HALF), F32),
            pltpu.VMEM((3, 2, ROWS, 128), BF16),
            pltpu.VMEM((3, 2, KEYS, 128), BF16),
            pltpu.VMEM((3, 2, KEYS, 128), BF16),
            pltpu.VMEM((ROWS, HALF), BF16),
            pltpu.VMEM((ZN, ROWS // ZN, HALF), BF16),
            pltpu.VMEM((ZN, ROWS // ZN, HALF), BF16),
            pltpu.VMEM((ROWS, HALF), BF16),
            pltpu.VMEM((ROWS, HALF), BF16),
            pltpu.VMEM((2, ROWS, HALF), BF16),
            pltpu.VMEM((2, ROWS, HALF), BF16),
            pltpu.VMEM((ROWS, D), F32),
            pltpu.SemaphoreType.DMA((8,)),
            pltpu.SemaphoreType.DMA((SENDS,)),
            pltpu.SemaphoreType.DMA((RECVS,)),
        ],
        compiler_params=pltpu.CompilerParams(
            collective_id=0, has_side_effects=True, vmem_limit_bytes=60 * 1024 * 1024
        ),
    )(
        trajectory, noise, mod_shift, mod_scale, step_size, prompt_table,
        prompt_map.reshape(1, ROWS), w_qkv, w_out.T,
    )
    return result[None]


def solution(mesh):
    return jax.shard_map(
        shards,
        mesh=mesh,
        in_specs=(
            P("step", "seg", None),
            P("seg", None),
            P("step", None),
            P("step", None),
            P("step"),
            P(),
            P("seg"),
            P(("seg", "step"), None),
            P(None, "step"),
        ),
        out_specs=P("step", "seg", None),
        check_vma=False,
    )
```

```python
import functools

import jax
import jax.numpy as jnp
from jax import lax
from jax.experimental import pallas as pl
from jax.experimental.pallas import tpu as pltpu
from jax.sharding import PartitionSpec as P

MESH = pl.DeviceIdType.MESH
BF16 = jnp.bfloat16
F32 = jnp.float32
XN, YN, ZN = 4, 8, 8
SEGS, STEPS = XN * YN, 2 * ZN
ROWS, HALO, D, HQ = 128, 64, 1536, 768
KEYS = ROWS + 2 * HALO
HALF = HQ // 2
CHUNKS = 9
SHARD = 3
BLOCK = SHARD * STEPS
SLOT = 32
WO = D // STEPS
PAIR = 2 * XN * BLOCK
SENDS, RECVS = 11, 89


def dot(a, b, contract=((1,), (0,)), precision=None):
    return lax.dot_general(a, b, (contract, ((), ())), preferred_element_type=F32, precision=precision)


class Net:
    def __init__(self, send, recv):
        self.sems, self.index, self.count = (send, recv), ({}, {}), {}

    def sem(self, side, name):
        index = self.index[side]
        return self.sems[side].at[index.setdefault(name, len(index))]

    def send(self, group, name, src, dst, device):
        self.count[group] = self.count.get(group, 0) + 1
        pltpu.make_async_remote_copy(
            src_ref=src, dst_ref=dst, send_sem=self.sem(0, group), recv_sem=self.sem(1, name),
            device_id=device, device_id_type=MESH,
        ).start()

    def wait(self, name, ref, device):
        pltpu.make_async_remote_copy(
            src_ref=ref, dst_ref=ref, send_sem=self.sems[0].at[0], recv_sem=self.sem(1, name),
            device_id=device, device_id_type=MESH,
        ).wait_recv()

    def sent(self, group, ref, device):
        pltpu.make_async_remote_copy(
            src_ref=ref, dst_ref=ref, send_sem=self.sem(0, group), recv_sem=self.sems[1].at[0],
            device_id=device, device_id_type=MESH,
        ).wait_send()


def kernel(
    traj_hbm, noise_hbm, shift_hbm, scale_hbm, size_hbm, table_hbm, pmap_hbm, wq_hbm, wo_hbm, out,
    traj, noise, shift, scale, size, table, pmap, wq, stage, shard, slots, perm, w, wt, mod, sizes,
    sum_q, sum_kv, q, k, v, own_t, parts, sums, before, give, full, extra, start, mask, load, send, recv,
):
    seg, step = lax.axis_index("seg"), lax.axis_index("step")
    x, y, core, z = lax.rem(seg, XN), lax.div(seg, XN), lax.rem(step, 2), lax.div(step, 2)
    other = 1 - core
    net = Net(send, recv)

    def ring(i, n):
        return lax.rem(i + n, n)

    def seg_of(dx, dy):
        return ring(y + dy, YN) * XN + ring(x + dx, XN)

    def at_seg(dx, dy):
        return (seg_of(dx, dy), step)

    def at_z(dz):
        return (seg, ring(z + dz, ZN) * 2 + core)

    sibling = (seg, z * 2 + other)
    following, preceding = (ring(seg + 1, SEGS), step), (ring(seg - 1, SEGS), step)

    peers = [(seg, ring(step + i, STEPS)) for i in range(1, STEPS)]
    peers += [at_seg(i, 0) for i in range(1, XN)] + [at_seg(0, i) for i in (1, -1, 2, -2)] + [following, preceding]
    barrier = pltpu.get_barrier_semaphore()
    for peer in peers:
        pl.semaphore_signal(barrier, inc=1, device_id=peer, device_id_type=MESH)

    near = lax.rem(x, 2)

    def wt_block(dz):
        return wt.at[near, ring(z + dz, ZN), core]

    sources = [
        (wq_hbm, wq), (traj_hbm, traj), (pmap_hbm, pmap), (table_hbm, table), (shift_hbm, shift), (scale_hbm, scale),
        (wo_hbm.at[:, pl.ds(pl.multiple_of(near * HALF, HALF), HALF)], wt_block(0)), (noise_hbm, noise),
        (size_hbm, size),
    ]
    loads = [pltpu.make_async_copy(src, dst, load.at[i]) for i, (src, dst) in enumerate(sources)]
    for copy in loads:
        copy.start()

    stage[...] = jnp.zeros_like(stage)
    loads[0].wait()
    rows = wq[...].astype(F32)
    for half in range(2):
        for c in range(CHUNKS):
            col = ((c // 3) * 6 + half * 3 + c % 3) * 128
            stage[half, c * SHARD : (c + 1) * SHARD, :] = rows[:, col : col + 128]
    shard[...] = stage[...].astype(BF16)
    slots[step] = shard[core]
    pl.semaphore_wait(barrier, len(peers))

    for dz in (4, 3, 5, 2, 6, 1, 7, 0):
        for swap in range(2):
            if (dz, swap) == (0, 0):
                continue
            there = lax.rem(core + swap, 2)
            net.send("z", "z", shard.at[there], slots.at[step], (seg, ring(z + dz, ZN) * 2 + there))

    def send_wz(way, far):
        if far + 1 < ZN // 2 or (far + 1 == ZN // 2 and way == 1):
            net.send("wz", ("wz", way, far + 1), wt_block(-way * far), wt_block(-way * far), at_z(way))

    def take_wz(way, far):
        net.wait(("wz", way, far), wt_block(-way * far), sibling)
        send_wz(way, far)

    mine, low, high = (slice(HALO, HALO + ROWS), slice(HALO, 2 * HALO), slice(ROWS, ROWS + HALO))
    first, last = slice(0, HALO), slice(HALO + ROWS, KEYS)
    for copy in loads[1:]:
        copy.wait()
    send_wz(1, 0)
    send_wz(-1, 0)
    whole = table[...]
    upper = whole.astype(BF16)
    rest = whole - upper.astype(F32)
    middle = rest.astype(BF16)
    lower = (rest - middle.astype(F32)).astype(BF16)
    onehot = (lax.broadcasted_iota(jnp.int32, (8, ROWS), 0) == pmap[...]).astype(F32)
    onehot = jnp.concatenate([onehot, onehot, onehot], axis=0).astype(BF16)
    chosen = dot(onehot, jnp.concatenate([upper, middle, lower], axis=0), ((0,), (0,)))
    inputs = traj[0].astype(F32) + chosen
    center = jnp.mean(inputs, axis=-1, keepdims=True)
    inputs = inputs - center
    spread = jnp.mean(jnp.square(inputs), axis=-1, keepdims=True)
    normed = inputs * lax.rsqrt(spread + 1e-06)
    mod[core, mine, :] = (normed * (1.0 + scale[...]) + shift[...]).astype(BF16)
    sizes[core] = jnp.broadcast_to(size[...], (8, 128))
    net.send("mod", "up", mod.at[core, high], mod.at[core, first], following)
    net.send("mod", "down", mod.at[core, low], mod.at[core, last], preceding)
    net.send("mod", "mod", mod.at[core, mine], mod.at[core, mine], sibling)
    net.send("size", "size", sizes.at[core], sizes.at[core], sibling)

    shape = (BLOCK, STEPS * SLOT)
    i = lax.broadcasted_iota(jnp.int32, shape, 0)
    third = lax.shift_right_logical(i * 43, 7)
    j = lax.broadcasted_iota(jnp.int32, shape, 1) - third * SLOT - (i - third * SHARD)
    for c in range(CHUNKS):
        perm[c * BLOCK : (c + 1) * BLOCK, :] = jnp.where(j == c * SHARD, 1.0, 0.0).astype(BF16)
    at_q = lax.broadcasted_iota(jnp.int32, (ROWS, KEYS), 0)
    at_k = lax.broadcasted_iota(jnp.int32, (ROWS, KEYS), 1)
    frame = seg * ROWS - HALO + at_k
    allowed = (at_k >= at_q) & (at_k <= at_q + 2 * HALO) & (frame >= 0) & (frame < SEGS * ROWS)
    mask[...] = jnp.where(allowed, 0.0, -1e30).astype(F32)
    net.wait("z", slots.at[0 : STEPS - 1], sibling)
    block = dot(perm[...], slots[...].reshape(STEPS * SLOT, 128)).astype(BF16)

    ours = 1 + lax.rem(z, 2)

    def part(which, dx, dy):
        return w.at[which, pl.ds(pl.multiple_of(seg_of(dx, dy) * BLOCK, BLOCK), BLOCK)]

    def blocks(n):
        return w.at[:, 0 : n * BLOCK // 3]

    for c in range(CHUNKS):
        own_rows = pl.ds(pl.multiple_of(seg * BLOCK, BLOCK), BLOCK)
        w[c // 3, own_rows, (c % 3) * 128 : (c % 3 + 1) * 128] = block[c * BLOCK : (c + 1) * BLOCK]

    def pass_on(name, ref, device):
        net.send("w", name, ref, ref, device)

    top = YN // 2

    def goes(way, far, is_b, dx=0):
        return far < top or (way == 1) == (is_b or dx % 2 == 0)

    def send_ax(dx):
        pass_on(("ax", -dx % XN), part(0, 0, 0), at_seg(dx, 0))

    def take_ax(dx):
        net.wait(("ax", dx % XN), part(0, dx, 0), sibling)
        send_ay(dx, 1, 0)
        send_ay(dx, -1, 0)

    def send_ay(dx, way, far):
        ref = part(0, dx, -way * far)
        if far + 1 < top:
            pass_on(("ay", dx, way, far + 1), ref, at_seg(0, way))
        if far + 2 == top and goes(way, top, False, dx):
            pass_on(("ay", dx, way, top), ref, at_seg(0, 2 * way))

    def take_ay(dx, far):
        for way in (1, -1):
            if goes(way, far, False, dx):
                net.wait(("ay", dx, way, far), part(0, dx, -way * far), sibling)
                send_ay(dx, way, far)

    def send_az(dx, dy):
        pass_on(("az", abs(dy)), part(ours, dx, dy), at_z(1 if dx % 2 == 0 else -1))

    def send_by(way, far, hops):
        if far + hops < top or goes(way, top, True):
            pass_on(("by", way, far + hops), part(ours, 0, -way * far), at_seg(0, hops * way))

    def take_by(far):
        for way in (1, -1):
            if goes(way, far, True):
                net.wait(("by", way, far), part(ours, 0, -way * far), sibling)
                if far == 2:
                    send_by(way, far, 1)
                    send_by(way, far, 2)
                send_bx(way, far)
                send_az(0, -way * far)

    def relayed(far):
        return 0 < far < top - 1

    def send_bx(way, far):
        for dx in (1, -1) if relayed(far) else (2, 1, -1):
            pass_on(("bx", -way * far, -dx % XN), part(ours, 0, -way * far), at_seg(dx, 0))

    def take_bx(far, opposite):
        for way in (1, -1):
            if not goes(way, far, True) or (far == 0 and way == -1):
                continue
            for dx in (2,) if opposite else (-way, way):
                ref = part(ours, dx, -way * far)
                net.wait(("bx", -way * far, dx % XN), ref, sibling)
                if relayed(far) and dx == -way:
                    pass_on(("bx", -way * far, 2), ref, at_seg(way, 0))
                send_az(dx, -way * far)

    def settle(far):
        net.wait(("az", far), blocks((2 if 0 < far < top else 1) * XN - (far == 0)), sibling)

    def project(pair, start):
        rows = pl.ds(pl.multiple_of(pair * PAIR, PAIR), PAIR)
        everyone = mod[:, :, rows].reshape(2 * KEYS, PAIR)
        asked = mod[:, mine, rows].reshape(2 * ROWS, PAIR)
        add_q, add_k, add_v = dot(asked, w[0, rows]), dot(everyone, w[1, rows]), dot(everyone, w[2, rows])
        sum_q[...] = add_q if start else sum_q[...] + add_q
        sum_kv[0] = add_k if start else sum_kv[0] + add_k
        sum_kv[1] = add_v if start else sum_kv[1] + add_v

    for dx in (1, -1, 2):
        send_ax(dx)
    for hops in (1, 2):
        send_by(1, 0, hops)
        send_by(-1, 0, hops)
    send_ay(0, 1, 0)
    send_ay(0, -1, 0)
    send_bx(1, 0)
    take_wz(1, 1)
    take_wz(-1, 1)

    pair = lax.div(y, 2)
    side = 1 - 2 * lax.rem(y, 2)
    pairs = [pair, ring(pair - side, YN // 2), ring(pair + side, YN // 2), ring(pair + 2, YN // 2)]

    for dx in (3, 1, 2):
        take_ax(dx)
    take_by(1)
    take_by(2)
    take_ay(0, 1)
    take_bx(0, False)
    net.wait("up", mod.at[core, first], sibling)
    net.send("mod", "mod", mod.at[core, first], mod.at[core, first], sibling)
    net.wait("down", mod.at[core, last], sibling)
    net.send("mod", "mod", mod.at[core, last], mod.at[core, last], sibling)
    take_wz(1, 2)
    take_wz(-1, 2)
    for dx in (3, 1, 2):
        take_ay(dx, 1)
    take_bx(1, False)
    take_bx(2, False)
    take_bx(0, True)
    take_by(3)
    take_by(4)
    take_wz(1, 3)
    take_wz(-1, 3)
    for dx in (0, 3, 1, 2):
        take_ay(dx, 2)
    take_bx(1, True)
    take_bx(2, True)
    for far in (3, 4):
        take_bx(far, False)
        take_bx(far, True)
    take_wz(1, 4)
    net.wait("mod", mod.at[other], sibling)
    net.wait("size", sizes.at[other], sibling)
    settle(0)
    settle(1)
    project(pairs[0], True)
    settle(2)
    project(pairs[1], False)
    for far in (3, 4):
        for dx in (0, 3, 1, 2):
            take_ay(dx, far)

    for way, zs in ((1, slice(0, ZN // 2)), (-1, slice(ZN // 2, ZN))):
        net.send("wx", "wx", wt.at[near, zs, core], wt.at[near, zs, core], at_seg(way, 0))
    net.send("ws", "ws", wt.at[near, :, core], wt.at[near, :, core], sibling)
    settle(top - 1)
    project(pairs[2], False)
    settle(top)
    project(pairs[3], False)
    for c in range(3):
        cols = slice(c * 128, (c + 1) * 128)
        q[c] = (sum_q[:, cols].astype(BF16) * 0.125).astype(BF16).reshape(2, ROWS, 128)
        k[c] = sum_kv[0, :, cols].astype(BF16).reshape(2, KEYS, 128)
        v[c] = sum_kv[1, :, cols].astype(BF16).reshape(2, KEYS, 128)

    share = ROWS // ZN

    def share_rows(i):
        return pl.ds(pl.multiple_of(i * share, share), share)

    bias = jnp.concatenate([mask[...], mask[...]], axis=0)
    lane = lax.broadcasted_iota(jnp.int32, (ROWS, 128), 1)
    ones = jnp.ones((KEYS, 128), BF16)
    for c in range(3):
        total = None
        for s in range(2):
            asked = q[c, s]
            nothing = jnp.zeros_like(asked)
            both = jnp.concatenate([jnp.where(lane < 64, asked, nothing), jnp.where(lane < 64, nothing, asked)], axis=0)
            scores = dot(both, k[c, s], ((1,), (1,))) + bias
            lifted = jnp.exp(scores - jnp.max(scores, axis=1, keepdims=True)).astype(BF16)
            got = dot(lifted, v[c, s]) / dot(lifted, ones)
            got = jnp.where(lane < 64, got[:ROWS], got[ROWS:]).astype(BF16)
            term = got.astype(F32) * sizes[s, 0:1, :]
            if s == 0:
                own_t[:, c * 128 : (c + 1) * 128] = term.astype(BF16)
                total = term
            else:
                total = total + term
        cols = slice(c * 128, (c + 1) * 128)
        give[:, cols] = total.astype(BF16)
        for dz in (4, 3, 5, 2, 6, 1, 7):
            there = share_rows(ring(z + dz, ZN))
            net.send("there", ("there", c), give.at[there, cols], parts.at[z, :, cols], at_z(dz))
        parts[z, :, cols] = give[share_rows(z), cols]

    net.send("own", "own", own_t, extra.at[core], sibling)
    for c in range(3):
        cols = slice(c * 128, (c + 1) * 128)
        net.wait(("there", c), parts.at[0 : ZN - 1, :, cols], sibling)
        total = jnp.zeros((share, 128), F32)
        for i in range(ZN):
            sums[i, :, cols] = total.astype(BF16)
            total = total + parts[i, :, cols].astype(F32)
        for dz in (4, 3, 5, 2, 6, 1, 7):
            there = ring(z + dz, ZN)
            net.send("back", ("back", c), sums.at[there, :, cols], before.at[share_rows(z), cols], at_z(dz))
        before[share_rows(z), cols] = sums[z, :, cols]

    net.wait("wx", wt.at[1 - near, :, core], sibling)
    net.send("ws", "ws", wt.at[1 - near, :, core], wt.at[1 - near, :, core], sibling)
    net.wait("ws", wt.at[:, :, other], sibling)
    net.wait("own", extra.at[other], sibling)
    odd = jnp.where(core == 0, jnp.zeros((ROWS, HALF), BF16), extra[other])
    base = dot(odd, wt[other].reshape(D, HALF), ((1,), (1,)))
    odd = jnp.where(core == 0, jnp.zeros((ROWS, HALF), BF16), own_t[...])
    start[...] = noise[...].astype(F32) + base + dot(odd, wt[core].reshape(D, HALF), ((1,), (1,)))

    for c in range(3):
        cols = slice(c * 128, (c + 1) * 128)
        net.wait(("back", c), before.at[0 : ROWS - share, cols], sibling)
        net.send("full", "full", before.at[:, cols], full.at[core, :, cols], sibling)
    start[...] += dot(before[...], wt[core].reshape(D, HALF), ((1,), (1,)))
    net.wait("full", full.at[other], sibling)
    out[...] = (start[...] + dot(full[other], wt[other].reshape(D, HALF), ((1,), (1,)))).astype(BF16)

    net.sent("z", slots.at[0 : STEPS - 1], sibling)
    net.sent("mod", mod.at[:, 0 : HALO + ROWS], sibling)
    net.sent("size", sizes.at[0], sibling)
    net.sent("w", blocks(net.count["w"]), sibling)
    net.sent("wz", wt.at[0, 0 : ZN - 1, 0], sibling)
    net.sent("wx", wt.at[0, :, 0], sibling)
    net.sent("ws", wt.at[:, :, 0], sibling)
    net.sent("there", parts.at[0 : ZN - 1], sibling)
    net.sent("back", parts.at[0 : ZN - 1], sibling)
    net.sent("own", own_t, sibling)
    net.sent("full", before, sibling)


def shards(trajectory, noise, mod_shift, mod_scale, step_size, prompt_table, prompt_map, w_qkv, w_out):
    vmem = pl.BlockSpec(memory_space=pltpu.VMEM)
    hbm = pl.BlockSpec(memory_space=pl.ANY)
    result = pl.pallas_call(
        kernel,
        out_shape=jax.ShapeDtypeStruct((ROWS, D), BF16),
        in_specs=[hbm] * 9,
        out_specs=vmem,
        scratch_shapes=[
            pltpu.VMEM((1, ROWS, D), BF16),
            pltpu.VMEM((ROWS, D), BF16),
            pltpu.VMEM((1, D), F32),
            pltpu.VMEM((1, D), F32),
            pltpu.VMEM((1, 1), F32),
            pltpu.VMEM((8, D), F32),
            pltpu.VMEM((1, ROWS), jnp.int32),
            pltpu.VMEM((SHARD, 3 * HQ), BF16),
            pltpu.VMEM((2, SLOT, 128), F32),
            pltpu.VMEM((2, SLOT, 128), BF16),
            pltpu.VMEM((STEPS, SLOT, 128), BF16),
            pltpu.VMEM((CHUNKS * BLOCK, STEPS * SLOT), BF16),
            pltpu.VMEM((3, D, HALF), BF16),
            pltpu.VMEM((2, ZN, 2, WO, HALF), BF16),
            pltpu.VMEM((2, KEYS, D), BF16),
            pltpu.VMEM((2, 8, 128), F32),
            pltpu.VMEM((2 * ROWS, HALF), F32),
            pltpu.VMEM((2, 2 * KEYS, HALF), F32),
            pltpu.VMEM((3, 2, ROWS, 128), BF16),
            pltpu.VMEM((3, 2, KEYS, 128), BF16),
            pltpu.VMEM((3, 2, KEYS, 128), BF16),
            pltpu.VMEM((ROWS, HALF), BF16),
            pltpu.VMEM((ZN, ROWS // ZN, HALF), BF16),
            pltpu.VMEM((ZN, ROWS // ZN, HALF), BF16),
            pltpu.VMEM((ROWS, HALF), BF16),
            pltpu.VMEM((ROWS, HALF), BF16),
            pltpu.VMEM((2, ROWS, HALF), BF16),
            pltpu.VMEM((2, ROWS, HALF), BF16),
            pltpu.VMEM((ROWS, D), F32),
            pltpu.VMEM((ROWS, KEYS), F32),
            pltpu.SemaphoreType.DMA((9,)),
            pltpu.SemaphoreType.DMA((SENDS,)),
            pltpu.SemaphoreType.DMA((RECVS,)),
        ],
        compiler_params=pltpu.CompilerParams(
            collective_id=0, has_side_effects=True, vmem_limit_bytes=60 * 1024 * 1024
        ),
    )(
        trajectory, noise, mod_shift, mod_scale, step_size.reshape(1, 1), prompt_table,
        prompt_map.reshape(1, ROWS), w_qkv, w_out.T,
    )
    return result[None]


def solution(mesh):
    return jax.shard_map(
        shards,
        mesh=mesh,
        in_specs=(
            P("step", "seg", None),
            P("seg", None),
            P("step", None),
            P("step", None),
            P("step"),
            P(),
            P("seg"),
            P(("seg", "step"), None),
            P(None, "step"),
        ),
        out_specs=P("step", "seg", None),
        check_vma=False,
    )
```

```python
import functools

import jax
import jax.numpy as jnp
from jax import lax
from jax.experimental import pallas as pl
from jax.experimental.pallas import tpu as pltpu
from jax.sharding import PartitionSpec as P

MESH = pl.DeviceIdType.MESH
BF16 = jnp.bfloat16
F32 = jnp.float32
XN, YN, ZN = 4, 8, 8
SEGS, STEPS = XN * YN, 2 * ZN
ROWS, HALO, D, HQ = 128, 64, 1536, 768
KEYS = ROWS + 2 * HALO
HALF = HQ // 2
CHUNKS = 9
SHARD = 3
BLOCK = SHARD * STEPS
SLOT = 32
WO = D // STEPS
PAIR = 2 * XN * BLOCK
SENDS, RECVS = 11, 89


def dot(a, b, contract=((1,), (0,)), precision=None):
    return lax.dot_general(a, b, (contract, ((), ())), preferred_element_type=F32, precision=precision)


class Net:
    def __init__(self, send, recv):
        self.sems, self.index, self.count = (send, recv), ({}, {}), {}

    def sem(self, side, name):
        index = self.index[side]
        return self.sems[side].at[index.setdefault(name, len(index))]

    def send(self, group, name, src, dst, device):
        self.count[group] = self.count.get(group, 0) + 1
        pltpu.make_async_remote_copy(
            src_ref=src, dst_ref=dst, send_sem=self.sem(0, group), recv_sem=self.sem(1, name),
            device_id=device, device_id_type=MESH,
        ).start()

    def wait(self, name, ref, device):
        pltpu.make_async_remote_copy(
            src_ref=ref, dst_ref=ref, send_sem=self.sems[0].at[0], recv_sem=self.sem(1, name),
            device_id=device, device_id_type=MESH,
        ).wait_recv()

    def sent(self, group, ref, device):
        pltpu.make_async_remote_copy(
            src_ref=ref, dst_ref=ref, send_sem=self.sem(0, group), recv_sem=self.sems[1].at[0],
            device_id=device, device_id_type=MESH,
        ).wait_send()


def kernel(
    traj_hbm, noise_hbm, shift_hbm, scale_hbm, size_hbm, table_hbm, pmap_hbm, wq_hbm, wo_hbm, out,
    traj, noise, shift, scale, size, table, pmap, wq, stage, shard, slots, perm, w, wt, mod, sizes,
    sum_q, sum_kv, q, k, v, own_t, parts, sums, before, give, full, extra, start, mask, load, send, recv,
):
    seg, step = lax.axis_index("seg"), lax.axis_index("step")
    x, y, core, z = lax.rem(seg, XN), lax.div(seg, XN), lax.rem(step, 2), lax.div(step, 2)
    other = 1 - core
    net = Net(send, recv)

    def ring(i, n):
        return lax.rem(i + n, n)

    def seg_of(dx, dy):
        return ring(y + dy, YN) * XN + ring(x + dx, XN)

    def at_seg(dx, dy):
        return (seg_of(dx, dy), step)

    def at_z(dz):
        return (seg, ring(z + dz, ZN) * 2 + core)

    sibling = (seg, z * 2 + other)
    following, preceding = (ring(seg + 1, SEGS), step), (ring(seg - 1, SEGS), step)

    peers = [(seg, ring(step + i, STEPS)) for i in range(1, STEPS)]
    peers += [at_seg(i, 0) for i in range(1, XN)] + [at_seg(0, i) for i in (1, -1, 2, -2)] + [following, preceding]
    barrier = pltpu.get_barrier_semaphore()
    for peer in peers:
        pl.semaphore_signal(barrier, inc=1, device_id=peer, device_id_type=MESH)

    near = lax.rem(x, 2)

    def wt_block(dz):
        return wt.at[near, ring(z + dz, ZN), core]

    sources = [
        (wq_hbm, wq), (traj_hbm, traj), (pmap_hbm, pmap), (table_hbm, table), (shift_hbm, shift), (scale_hbm, scale),
        (wo_hbm.at[:, pl.ds(pl.multiple_of(near * HALF, HALF), HALF)], wt_block(0)), (noise_hbm, noise),
        (size_hbm, size),
    ]
    loads = [pltpu.make_async_copy(src, dst, load.at[i]) for i, (src, dst) in enumerate(sources)]
    for copy in loads:
        copy.start()

    stage[...] = jnp.zeros_like(stage)
    loads[0].wait()
    rows = wq[...].astype(F32)
    for half in range(2):
        for c in range(CHUNKS):
            col = ((c // 3) * 6 + half * 3 + c % 3) * 128
            stage[half, c * SHARD : (c + 1) * SHARD, :] = rows[:, col : col + 128]
    shard[...] = stage[...].astype(BF16)
    slots[step] = shard[core]
    pl.semaphore_wait(barrier, len(peers))

    for dz in (4, 3, 5, 2, 6, 1, 7, 0):
        for swap in range(2):
            if (dz, swap) == (0, 0):
                continue
            there = lax.rem(core + swap, 2)
            net.send("z", "z", shard.at[there], slots.at[step], (seg, ring(z + dz, ZN) * 2 + there))

    def send_wz(way, far):
        if far + 1 < ZN // 2 or (far + 1 == ZN // 2 and way == 1):
            net.send("wz", ("wz", way, far + 1), wt_block(-way * far), wt_block(-way * far), at_z(way))

    def take_wz(way, far):
        net.wait(("wz", way, far), wt_block(-way * far), sibling)
        send_wz(way, far)

    mine, low, high = (slice(HALO, HALO + ROWS), slice(HALO, 2 * HALO), slice(ROWS, ROWS + HALO))
    first, last = slice(0, HALO), slice(HALO + ROWS, KEYS)
    for copy in loads[1:]:
        copy.wait()
    send_wz(1, 0)
    send_wz(-1, 0)
    whole = table[...]
    upper = whole.astype(BF16)
    rest = whole - upper.astype(F32)
    middle = rest.astype(BF16)
    lower = (rest - middle.astype(F32)).astype(BF16)
    onehot = (lax.broadcasted_iota(jnp.int32, (8, ROWS), 0) == pmap[...]).astype(F32)
    onehot = jnp.concatenate([onehot, onehot, onehot], axis=0).astype(BF16)
    chosen = dot(onehot, jnp.concatenate([upper, middle, lower], axis=0), ((0,), (0,)))
    inputs = traj[0].astype(F32) + chosen
    center = jnp.mean(inputs, axis=-1, keepdims=True)
    inputs = inputs - center
    spread = jnp.mean(jnp.square(inputs), axis=-1, keepdims=True)
    normed = inputs * lax.rsqrt(spread + 1e-06)
    mod[core, mine, :] = (normed * (1.0 + scale[...]) + shift[...]).astype(BF16)
    sizes[core] = jnp.broadcast_to(size[...], (8, 128))
    net.send("mod", "up", mod.at[core, high], mod.at[core, first], following)
    net.send("mod", "down", mod.at[core, low], mod.at[core, last], preceding)
    net.send("mod", "mod", mod.at[core, mine], mod.at[core, mine], sibling)
    net.send("size", "size", sizes.at[core], sizes.at[core], sibling)

    shape = (BLOCK, STEPS * SLOT)
    i = lax.broadcasted_iota(jnp.int32, shape, 0)
    third = lax.shift_right_logical(i * 43, 7)
    j = lax.broadcasted_iota(jnp.int32, shape, 1) - third * SLOT - (i - third * SHARD)
    for c in range(CHUNKS):
        perm[c * BLOCK : (c + 1) * BLOCK, :] = jnp.where(j == c * SHARD, 1.0, 0.0).astype(BF16)
    at_q = lax.broadcasted_iota(jnp.int32, (ROWS, KEYS), 0)
    at_k = lax.broadcasted_iota(jnp.int32, (ROWS, KEYS), 1)
    frame = seg * ROWS - HALO + at_k
    allowed = (at_k >= at_q) & (at_k <= at_q + 2 * HALO) & (frame >= 0) & (frame < SEGS * ROWS)
    mask[...] = jnp.where(allowed, 0.0, -1e30).astype(F32)
    net.wait("z", slots.at[0 : STEPS - 1], sibling)
    block = dot(perm[...], slots[...].reshape(STEPS * SLOT, 128)).astype(BF16)

    ours = 1 + lax.rem(z, 2)

    def part(which, dx, dy):
        return w.at[which, pl.ds(pl.multiple_of(seg_of(dx, dy) * BLOCK, BLOCK), BLOCK)]

    def blocks(n):
        return w.at[:, 0 : n * BLOCK // 3]

    for c in range(CHUNKS):
        own_rows = pl.ds(pl.multiple_of(seg * BLOCK, BLOCK), BLOCK)
        w[c // 3, own_rows, (c % 3) * 128 : (c % 3 + 1) * 128] = block[c * BLOCK : (c + 1) * BLOCK]

    def pass_on(name, ref, device):
        net.send("w", name, ref, ref, device)

    top = YN // 2

    def goes(way, far, is_b, dx=0):
        return far < top or (way == 1) == (is_b or dx % 2 == 0)

    def send_ax(dx):
        pass_on(("ax", -dx % XN), part(0, 0, 0), at_seg(dx, 0))

    def take_ax(dx):
        net.wait(("ax", dx % XN), part(0, dx, 0), sibling)
        send_ay(dx, 1, 0)
        send_ay(dx, -1, 0)

    def send_ay(dx, way, far):
        ref = part(0, dx, -way * far)
        if far + 1 < top:
            pass_on(("ay", dx, way, far + 1), ref, at_seg(0, way))
        if far + 2 == top and goes(way, top, False, dx):
            pass_on(("ay", dx, way, top), ref, at_seg(0, 2 * way))

    def take_ay(dx, far):
        for way in (1, -1):
            if goes(way, far, False, dx):
                net.wait(("ay", dx, way, far), part(0, dx, -way * far), sibling)
                send_ay(dx, way, far)

    def send_az(dx, dy):
        pass_on(("az", abs(dy)), part(ours, dx, dy), at_z(1 if dx % 2 == 0 else -1))

    def send_by(way, far, hops):
        if far + hops < top or goes(way, top, True):
            pass_on(("by", way, far + hops), part(ours, 0, -way * far), at_seg(0, hops * way))

    def take_by(far):
        for way in (1, -1):
            if goes(way, far, True):
                net.wait(("by", way, far), part(ours, 0, -way * far), sibling)
                if far == 2:
                    send_by(way, far, 1)
                    send_by(way, far, 2)
                send_bx(way, far)
                send_az(0, -way * far)

    def relayed(far):
        return 0 < far < top - 1

    def send_bx(way, far):
        for dx in (1, -1) if relayed(far) else (2, 1, -1):
            pass_on(("bx", -way * far, -dx % XN), part(ours, 0, -way * far), at_seg(dx, 0))

    def take_bx(far, opposite):
        for way in (1, -1):
            if not goes(way, far, True) or (far == 0 and way == -1):
                continue
            for dx in (2,) if opposite else (-way, way):
                ref = part(ours, dx, -way * far)
                net.wait(("bx", -way * far, dx % XN), ref, sibling)
                if relayed(far) and dx == -way:
                    pass_on(("bx", -way * far, 2), ref, at_seg(way, 0))
                send_az(dx, -way * far)

    def settle(far):
        net.wait(("az", far), blocks((2 if 0 < far < top else 1) * XN - (far == 0)), sibling)

    def project(pair, start):
        rows = pl.ds(pl.multiple_of(pair * PAIR, PAIR), PAIR)
        everyone = mod[:, :, rows].reshape(2 * KEYS, PAIR)
        asked = mod[:, mine, rows].reshape(2 * ROWS, PAIR)
        add_q, add_k, add_v = dot(asked, w[0, rows]), dot(everyone, w[1, rows]), dot(everyone, w[2, rows])
        sum_q[...] = add_q if start else sum_q[...] + add_q
        sum_kv[0] = add_k if start else sum_kv[0] + add_k
        sum_kv[1] = add_v if start else sum_kv[1] + add_v

    for dx in (1, -1, 2):
        send_ax(dx)
    for hops in (1, 2):
        send_by(1, 0, hops)
        send_by(-1, 0, hops)
    send_ay(0, 1, 0)
    send_ay(0, -1, 0)
    send_bx(1, 0)
    take_wz(1, 1)
    take_wz(-1, 1)

    pair = lax.div(y, 2)
    side = 1 - 2 * lax.rem(y, 2)
    pairs = [pair, ring(pair - side, YN // 2), ring(pair + side, YN // 2), ring(pair + 2, YN // 2)]

    for dx in (3, 1, 2):
        take_ax(dx)
    take_by(1)
    take_by(2)
    take_ay(0, 1)
    take_bx(0, False)
    net.wait("up", mod.at[core, first], sibling)
    net.send("mod", "mod", mod.at[core, first], mod.at[core, first], sibling)
    net.wait("down", mod.at[core, last], sibling)
    net.send("mod", "mod", mod.at[core, last], mod.at[core, last], sibling)
    take_wz(1, 2)
    take_wz(-1, 2)
    for dx in (3, 1, 2):
        take_ay(dx, 1)
    take_bx(1, False)
    take_bx(2, False)
    take_bx(0, True)
    take_by(3)
    take_by(4)
    take_wz(1, 3)
    take_wz(-1, 3)
    for dx in (0, 3, 1, 2):
        take_ay(dx, 2)
    take_bx(1, True)
    take_bx(2, True)
    for far in (3, 4):
        take_bx(far, False)
        take_bx(far, True)
    take_wz(1, 4)
    net.wait("mod", mod.at[other], sibling)
    net.wait("size", sizes.at[other], sibling)
    settle(0)
    settle(1)
    project(pairs[0], True)
    settle(2)
    project(pairs[1], False)
    for far in (3, 4):
        for dx in (0, 3, 1, 2):
            take_ay(dx, far)

    for way, zs in ((1, slice(0, ZN // 2)), (-1, slice(ZN // 2, ZN))):
        net.send("wx", "wx", wt.at[near, zs, core], wt.at[near, zs, core], at_seg(way, 0))
    net.send("ws", "ws", wt.at[near, :, core], wt.at[near, :, core], sibling)
    settle(top - 1)
    project(pairs[2], False)
    settle(top)
    project(pairs[3], False)
    for c in range(3):
        cols = slice(c * 128, (c + 1) * 128)
        q[c] = (sum_q[:, cols].astype(BF16) * 0.125).astype(BF16).reshape(2, ROWS, 128)
        k[c] = sum_kv[0, :, cols].astype(BF16).reshape(2, KEYS, 128)
        v[c] = sum_kv[1, :, cols].astype(BF16).reshape(2, KEYS, 128)

    share = ROWS // ZN

    def share_rows(i):
        return pl.ds(pl.multiple_of(i * share, share), share)

    bias = jnp.concatenate([mask[...], mask[...]], axis=0)
    lane = lax.broadcasted_iota(jnp.int32, (ROWS, 128), 1)
    ones = jnp.ones((KEYS, 128), BF16)
    for c in range(3):
        total = None
        for s in range(2):
            asked = q[c, s]
            nothing = jnp.zeros_like(asked)
            both = jnp.concatenate([jnp.where(lane < 64, asked, nothing), jnp.where(lane < 64, nothing, asked)], axis=0)
            scores = dot(both, k[c, s], ((1,), (1,))) + bias
            lifted = jnp.exp(scores - jnp.max(scores, axis=1, keepdims=True)).astype(BF16)
            got = dot(lifted, v[c, s]) / dot(lifted, ones)
            got = jnp.where(lane < 64, got[:ROWS], got[ROWS:]).astype(BF16)
            term = got.astype(F32) * sizes[s, 0:1, :]
            if s == 0:
                own_t[:, c * 128 : (c + 1) * 128] = term.astype(BF16)
                total = term
            else:
                total = total + term
        cols = slice(c * 128, (c + 1) * 128)
        give[:, cols] = total.astype(BF16)
        for dz in (4, 3, 5, 2, 6, 1, 7):
            there = share_rows(ring(z + dz, ZN))
            net.send("there", ("there", c), give.at[there, cols], parts.at[z, :, cols], at_z(dz))
        parts[z, :, cols] = give[share_rows(z), cols]

    net.send("own", "own", own_t, extra.at[core], sibling)
    for c in range(3):
        cols = slice(c * 128, (c + 1) * 128)
        net.wait(("there", c), parts.at[0 : ZN - 1, :, cols], sibling)
        total = jnp.zeros((share, 128), F32)
        for i in range(ZN):
            sums[i, :, cols] = total.astype(BF16)
            total = total + parts[i, :, cols].astype(F32)
        for dz in (4, 3, 5, 2, 6, 1, 7):
            there = ring(z + dz, ZN)
            net.send("back", ("back", c), sums.at[there, :, cols], before.at[share_rows(z), cols], at_z(dz))
        before[share_rows(z), cols] = sums[z, :, cols]

    net.wait("wx", wt.at[1 - near, :, core], sibling)
    net.send("ws", "ws", wt.at[1 - near, :, core], wt.at[1 - near, :, core], sibling)
    net.wait("ws", wt.at[:, :, other], sibling)
    net.wait("own", extra.at[other], sibling)
    odd = jnp.where(core == 0, jnp.zeros((ROWS, HALF), BF16), extra[other])
    base = dot(odd, wt[other].reshape(D, HALF), ((1,), (1,)))
    odd = jnp.where(core == 0, jnp.zeros((ROWS, HALF), BF16), own_t[...])
    start[...] = noise[...].astype(F32) + base + dot(odd, wt[core].reshape(D, HALF), ((1,), (1,)))

    for c in range(3):
        cols = slice(c * 128, (c + 1) * 128)
        net.wait(("back", c), before.at[0 : ROWS - share, cols], sibling)
        net.send("full", "full", before.at[:, cols], full.at[core, :, cols], sibling)
    start[...] += dot(before[...], wt[core].reshape(D, HALF), ((1,), (1,)))
    net.wait("full", full.at[other], sibling)
    out[...] = (start[...] + dot(full[other], wt[other].reshape(D, HALF), ((1,), (1,)))).astype(BF16)

    net.sent("z", slots.at[0 : STEPS - 1], sibling)
    net.sent("mod", mod.at[:, 0 : HALO + ROWS], sibling)
    net.sent("size", sizes.at[0], sibling)
    net.sent("w", blocks(net.count["w"]), sibling)
    net.sent("wz", wt.at[0, 0 : ZN - 1, 0], sibling)
    net.sent("wx", wt.at[0, :, 0], sibling)
    net.sent("ws", wt.at[:, :, 0], sibling)
    net.sent("there", parts.at[0 : ZN - 1], sibling)
    net.sent("back", parts.at[0 : ZN - 1], sibling)
    net.sent("own", own_t, sibling)
    net.sent("full", before, sibling)


def hand_over(result, out):
    out[0] = result[...]


def shards(trajectory, noise, mod_shift, mod_scale, step_size, prompt_table, prompt_map, w_qkv, w_out):
    vmem = pl.BlockSpec(memory_space=pltpu.VMEM)
    hbm = pl.BlockSpec(memory_space=pl.ANY)
    result = pl.pallas_call(
        kernel,
        out_shape=jax.ShapeDtypeStruct((ROWS, D), BF16),
        in_specs=[hbm] * 9,
        out_specs=vmem,
        scratch_shapes=[
            pltpu.VMEM((1, ROWS, D), BF16),
            pltpu.VMEM((ROWS, D), BF16),
            pltpu.VMEM((1, D), F32),
            pltpu.VMEM((1, D), F32),
            pltpu.VMEM((1, 1), F32),
            pltpu.VMEM((8, D), F32),
            pltpu.VMEM((1, ROWS), jnp.int32),
            pltpu.VMEM((SHARD, 3 * HQ), BF16),
            pltpu.VMEM((2, SLOT, 128), F32),
            pltpu.VMEM((2, SLOT, 128), BF16),
            pltpu.VMEM((STEPS, SLOT, 128), BF16),
            pltpu.VMEM((CHUNKS * BLOCK, STEPS * SLOT), BF16),
            pltpu.VMEM((3, D, HALF), BF16),
            pltpu.VMEM((2, ZN, 2, WO, HALF), BF16),
            pltpu.VMEM((2, KEYS, D), BF16),
            pltpu.VMEM((2, 8, 128), F32),
            pltpu.VMEM((2 * ROWS, HALF), F32),
            pltpu.VMEM((2, 2 * KEYS, HALF), F32),
            pltpu.VMEM((3, 2, ROWS, 128), BF16),
            pltpu.VMEM((3, 2, KEYS, 128), BF16),
            pltpu.VMEM((3, 2, KEYS, 128), BF16),
            pltpu.VMEM((ROWS, HALF), BF16),
            pltpu.VMEM((ZN, ROWS // ZN, HALF), BF16),
            pltpu.VMEM((ZN, ROWS // ZN, HALF), BF16),
            pltpu.VMEM((ROWS, HALF), BF16),
            pltpu.VMEM((ROWS, HALF), BF16),
            pltpu.VMEM((2, ROWS, HALF), BF16),
            pltpu.VMEM((2, ROWS, HALF), BF16),
            pltpu.VMEM((ROWS, D), F32),
            pltpu.VMEM((ROWS, KEYS), F32),
            pltpu.SemaphoreType.DMA((9,)),
            pltpu.SemaphoreType.DMA((SENDS,)),
            pltpu.SemaphoreType.DMA((RECVS,)),
        ],
        compiler_params=pltpu.CompilerParams(
            collective_id=0, has_side_effects=True, vmem_limit_bytes=60 * 1024 * 1024
        ),
    )(
        trajectory, noise, mod_shift, mod_scale, step_size.reshape(1, 1), prompt_table,
        prompt_map.reshape(1, ROWS), w_qkv, w_out.T,
    )
    rows = ROWS // 4
    return pl.pallas_call(
        hand_over,
        grid=(4,),
        out_shape=jax.ShapeDtypeStruct((1, ROWS, D), BF16),
        in_specs=[pl.BlockSpec((rows, D), lambda i: (i, 0))],
        out_specs=pl.BlockSpec((1, rows, D), lambda i: (0, i, 0)),
        compiler_params=pltpu.CompilerParams(vmem_limit_bytes=60 * 1024 * 1024),
    )(result)


def solution(mesh):
    return jax.shard_map(
        shards,
        mesh=mesh,
        in_specs=(
            P("step", "seg", None),
            P("seg", None),
            P("step", None),
            P("step", None),
            P("step"),
            P(),
            P("seg"),
            P(("seg", "step"), None),
            P(None, "step"),
        ),
        out_specs=P("step", "seg", None),
        check_vma=False,
    )
```
